256 devices in a mesh: dp: 16 (over y, z_lo), tensor: 16 (over x, z_hi, core).
Axes of the slice: x: 4, y: 4, z: 8 (z_hi: 2, z_lo: 4; z = z_hi * 4 + z_lo), core: 2. Of those that a mesh axis runs over, the one named last changes fastest.
Arguments:
- activations: bfloat16 [8192, 4096], P(('dp', 'tensor')), may hold values from -24 to 24
- token_scales: float32 [8192], P(('dp', 'tensor')), may hold values from 0.3 to 3
- out_grad: bfloat16 [8192, 14336], P('dp', 'tensor'), may hold values from -6 to 6
- weight: bfloat16 [4096, 14336], P('dp', 'tensor'), may hold values from -0.09375 to 0.09375
- logits: float32 [6, 1024, 14336], P(None, 'dp', 'tensor'), may hold values from -8 to 8
- gumbel: float32 [6, 1024, 14336], P(None, 'dp', 'tensor'), may hold values from -2.7 to 13.9, as said below
Outputs:
- input_grad: bfloat16 [8192, 4096], P(('dp', 'tensor'))
- logit_grad: float32 [6, 1024, 14336], P(None, 'dp', 'tensor')
The draws below stay inside these ranges and needn't reach their ends.
Inputs may be any that keep to these rules, and one draw needn't show every extreme that they name: `gumbel`: entries are independent.
All inputs are finite; a program needn't handle non-finite values.
Results may differ from the reference program's by a relative error of at most 0.0049.
Values may be sent and summed in bfloat16 or wider, within the bound.
No kernel may reach another device: no remote copies, remote signals or barrier semaphores. Data moves between devices by JAX's collectives and lax.ppermute only.
A program may use at most 128 MiB of HBM per device.

```python
import math
import jax
import jax.numpy as jnp

D = 4096
FF = 14336
TOKENS = 8192
GROUPS = 1024


def draw_gumbel(key, part):
    key = jax.random.fold_in(key, 7)
    uniform_draw = jax.random.uniform(key, (6, GROUPS, FF), jnp.float32, 1e-06, 1.0 - 1e-06)
    return -jnp.log(-jnp.log(uniform_draw))


def with_spikes(drawn, own_key, source, target, shards_of, factor):
    def block_of(dim):
        return (jnp.arange(drawn.shape[dim]) // (drawn.shape[dim] // shards_of)).reshape((-1,) + (1,) * (drawn.ndim - 1 - dim))

    first = jax.random.permutation(own_key, shards_of)[block_of(target)]
    second = (block_of(target) + shards_of // 2) % shards_of
    return jnp.where((block_of(source) == first) | (block_of(source) == second), factor * drawn, drawn)


def shard_levels(own_key, extent, cuts, least, largest):
    loudness, own = 1.0, jax.random.fold_in(own_key, 6)
    for dim, shards_of in cuts:
        heights = jnp.exp(jax.random.uniform(jax.random.fold_in(own, dim), (shards_of,), jnp.float32, least / len(cuts), largest / len(cuts)))
        loudness = loudness * jnp.repeat(heights, extent[dim] // shards_of).reshape([-1 if axis == dim else 1 for axis in range(len(extent))])
    return loudness


def gaussian(stream_key, shape, spread, bound, shards=(), held_as=jnp.bfloat16):
    drawn = spread * jax.random.normal(stream_key, shape, jnp.float32)
    if shards:
        drawn = drawn * shard_levels(stream_key, shape, shards, -0.22, 0.18)
    return jnp.clip(drawn, -bound, bound).astype(held_as)


def noise_with(key, extent, deviation, most, shards, heavy, kind=jnp.bfloat16):
    entries = deviation * jax.random.normal(key, extent, jnp.float32)
    if shards:
        entries = entries * shard_levels(key, extent, shards, -0.22, 0.18)
    return jnp.clip(with_spikes(entries, jax.random.fold_in(key, 3), *heavy), -most, most).astype(kind)


def setup_inputs(seed: int = 0) -> dict:
    key_of = jax.random.split(jax.random.key(seed), 7)
    activations = noise_with(key_of[0], (TOKENS, D), 1.0, 24.0, ((0, 256),), (0, 1, 256, 6.0))
    token_scales = jnp.clip(jnp.exp(math.log(3.0) - 2.3025851 * jax.random.uniform(key_of[1], (TOKENS,), jnp.float32) ** shard_levels(key_of[1], (TOKENS,), ((0, 256),), -0.2, 0.2)), 0.3, 3.0)
    out_grad = gaussian(key_of[2], (TOKENS, FF), 1.0, 6.0, ((0, 16), (1, 16)))
    weight = gaussian(key_of[3], (D, FF), D ** -0.5, 0.09375, ((0, 16), (1, 16)))
    logits = gaussian(key_of[4], (6, GROUPS, FF), 2.0, 8.0, ((1, 16), (2, 16)), jnp.float32)
    gumbel = draw_gumbel(jax.random.fold_in(key_of[6], 71), 0)
    return dict(activations=activations, token_scales=token_scales, out_grad=out_grad, weight=weight, logits=logits, gumbel=gumbel)


PATTERN_PAIRS = ((0, 1), (0, 2), (0, 3), (1, 2), (1, 3), (2, 3))
inverse_temp = 0.5


def soft_mask(logits, gumbel):
    exponent = jnp.exp((logits + gumbel) * inverse_temp)
    chances = exponent / jnp.sum(exponent, axis=0)
    kept_slots = []
    for position in range(4):
        chosen = [chances[which] for which in range(6) if position in PATTERN_PAIRS[which]]
        kept_slots.append(chosen[0] + chosen[1] + chosen[2])
    mask_full = jnp.stack(kept_slots, axis=1)
    return chances, mask_full.reshape(-1, mask_full.shape[2])


def logit_grads(chances, mask_grad):
    groups = mask_grad.reshape(-1, 4, mask_grad.shape[1])
    pattern = jnp.stack([groups[:, first_slot] + groups[:, second_slot] for first_slot, second_slot in PATTERN_PAIRS], axis=0)
    average = jnp.sum(chances * pattern, axis=0)
    return chances * (pattern - average) * inverse_temp


def reference(activations, token_scales, out_grad, weight, logits, gumbel):
    scaled = (activations.astype(jnp.float32) * token_scales[:, None]).astype(jnp.bfloat16)
    chances, mask_full = soft_mask(logits, gumbel)
    masked = (weight.astype(jnp.float32) * mask_full).astype(jnp.bfloat16)
    input_grad = jnp.dot(out_grad, masked.T, preferred_element_type=jnp.float32).astype(jnp.bfloat16)
    grad_full = jnp.dot(scaled.T, out_grad, preferred_element_type=jnp.float32)
    mask_grad = grad_full * weight.astype(jnp.float32)
    return input_grad, logit_grads(chances, mask_grad)
```

```python
import jax
import jax.numpy as jnp
from jax import lax
from jax.sharding import Mesh, PartitionSpec as P

PATTERN_PAIRS = ((0, 1), (0, 2), (0, 3), (1, 2), (1, 3), (2, 3))
inverse_temp = 0.5
F32, BF16 = jnp.float32, jnp.bfloat16


def soft_mask(logits, gumbel):
    exponent = jnp.exp((logits + gumbel) * inverse_temp)
    chances = exponent / jnp.sum(exponent, axis=0)
    kept_slots = []
    for position in range(4):
        chosen = [chances[which] for which in range(6) if position in PATTERN_PAIRS[which]]
        kept_slots.append(chosen[0] + chosen[1] + chosen[2])
    mask_full = jnp.stack(kept_slots, axis=1)
    return (chances, mask_full.reshape(-1, mask_full.shape[2]))


def logit_grads(chances, mask_grad):
    groups = mask_grad.reshape(-1, 4, mask_grad.shape[1])
    pattern = jnp.stack(
        [
            groups[:, first_slot] + groups[:, second_slot]
            for first_slot, second_slot in PATTERN_PAIRS
        ],
        axis=0,
    )
    average = jnp.sum(chances * pattern, axis=0)
    return chances * (pattern - average) * inverse_temp


def shift(value, axis, by):
    size = lax.axis_size(axis)
    return lax.ppermute(value, axis, [(i, (i + by) % size) for i in range(size)])


def body(activations, token_scales, out_grad, weight, logits, gumbel):
    y, zl, x = lax.axis_index("y"), lax.axis_index("zl"), lax.axis_index("x")
    zh, core = lax.axis_index("zh"), lax.axis_index("c")
    rows, features = activations.shape
    depth, hidden = weight.shape
    wide = 4 * depth

    blocks = out_grad.reshape(4, 2, 2, rows, hidden)
    blocks = jnp.where(core == 0, blocks, blocks[:, :, ::-1])
    blocks = jnp.where(zh == 0, blocks, blocks[:, ::-1])
    blocks = jnp.concatenate(
        [lax.dynamic_slice_in_dim(blocks, (x - j) % 4, 1, 0) for j in range(4)], axis=0
    )
    own = blocks.transpose(2, 0, 1, 3, 4).reshape(16 * rows, hidden)
    half = 8 * rows

    local = (activations.astype(F32) * token_scales[:, None]).astype(BF16)
    pieces = []
    for k in range(4):
        pieces.append(
            jnp.concatenate(
                [
                    lax.dynamic_slice_in_dim(
                        local, ((y + k) % 4) * wide + ((zl - m) % 4) * depth, depth, 1
                    )
                    for m in range(4)
                ],
                axis=1,
            )
        )
    scaled = jnp.stack([pieces[0]] + [shift(pieces[k], "y", k) for k in (1, 2, 3)], axis=0)

    chances, mask_full = soft_mask(logits, gumbel)
    weight_wide = weight.astype(F32)
    masked = (weight_wide * mask_full).astype(BF16)

    below = shift(own, "y", 1)
    above = shift(own, "y", -1)
    far = jnp.concatenate([shift(below[:half], "y", 1), shift(above[half:], "y", -1)], axis=0)
    grads = jnp.stack([own, below, far, above], axis=0)

    scaled = jnp.stack([scaled, shift(scaled, "zh", 1)], axis=0)
    scaled = jnp.stack([scaled] + [shift(scaled, "x", j) for j in (1, 2, 3)], axis=0)
    scaled = jnp.stack([scaled, shift(scaled, "c", 1)], axis=0)
    scaled = scaled.transpose(3, 0, 1, 2, 4, 5).reshape(4 * 16 * rows, wide)

    held = [masked]
    for _ in range(3):
        held.append(shift(held[-1], "zl", 1))
    masked_wide = jnp.concatenate(held, axis=0)

    grad_w = lax.dot_general(
        scaled,
        grads.reshape(4 * 16 * rows, hidden),
        (((0,), (0,)), ((), ())),
        preferred_element_type=F32,
    ).reshape(4, depth, hidden)
    moving = grad_w[1].astype(BF16)
    for m in (2, 3):
        moving = (shift(moving, "zl", 1).astype(F32) + grad_w[m]).astype(BF16)
    grad_own = shift(moving, "zl", 1).astype(F32) + grad_w[0]

    grads = grads.reshape(4, 2, 4, 2 * rows, hidden)
    kept = lax.dot_general(
        grads[:, 0], masked_wide, (((3,), (1,)), ((), ())), preferred_element_type=F32
    )
    given = lax.dot_general(
        grads[:, 1], masked_wide, (((3,), (1,)), ((), ())), preferred_element_type=F32
    ).astype(BF16)
    total = kept + shift(given, "c", 1).astype(F32)
    sent = total.astype(BF16)
    total = total[:, 0]
    for j in (1, 2, 3):
        total = total + shift(sent[:, j], "x", -j).astype(F32)
    total = total.reshape(4, 2, rows, wide)
    total = total[:, 0] + shift(total[:, 1].astype(BF16), "zh", 1).astype(F32)
    total = total.astype(BF16)
    parts = [total[0]] + [shift(total[k], "y", -k) for k in (1, 2, 3)]
    parts = jnp.stack(parts, axis=1)
    parts = jnp.concatenate(
        [lax.dynamic_slice_in_dim(parts, (q - y) % 4, 1, 1) for q in range(4)], axis=1
    ).reshape(rows, 4, 4, depth)
    parts = jnp.concatenate(
        [lax.dynamic_slice_in_dim(parts, (zl - q) % 4, 1, 2) for q in range(4)], axis=2
    )
    input_grad = parts.reshape(rows, features)

    return (input_grad, logit_grads(chances, grad_own * weight_wide))


def solution(mesh):
    fine = Mesh(mesh.devices.reshape(4, 4, 4, 2, 2), ("y", "zl", "x", "zh", "c"))
    dp, tensor = ("y", "zl"), ("x", "zh", "c")
    return jax.shard_map(
        body,
        mesh=fine,
        in_specs=(
            P(dp + tensor, None),
            P(dp + tensor),
            P(dp, tensor),
            P(dp, tensor),
            P(None, dp, tensor),
            P(None, dp, tensor),
        ),
        out_specs=(P(dp + tensor, None), P(None, dp, tensor)),
        check_vma=False,
    )
```

```python
import jax
import jax.numpy as jnp
from jax import lax
from jax.sharding import Mesh, PartitionSpec as P

PATTERN_PAIRS = ((0, 1), (0, 2), (0, 3), (1, 2), (1, 3), (2, 3))
inverse_temp = 0.5
F32, BF16 = jnp.float32, jnp.bfloat16


def soft_mask(logits, gumbel):
    exponent = jnp.exp((logits + gumbel) * inverse_temp)
    chances = exponent / jnp.sum(exponent, axis=0)
    kept_slots = []
    for position in range(4):
        chosen = [chances[which] for which in range(6) if position in PATTERN_PAIRS[which]]
        kept_slots.append(chosen[0] + chosen[1] + chosen[2])
    mask_full = jnp.stack(kept_slots, axis=1)
    return (chances, mask_full.reshape(-1, mask_full.shape[2]))


def logit_grads(chances, mask_grad):
    groups = mask_grad.reshape(-1, 4, mask_grad.shape[1])
    pattern = jnp.stack(
        [
            groups[:, first_slot] + groups[:, second_slot]
            for first_slot, second_slot in PATTERN_PAIRS
        ],
        axis=0,
    )
    average = jnp.sum(chances * pattern, axis=0)
    return chances * (pattern - average) * inverse_temp


def shift(value, axis, by):
    size = lax.axis_size(axis)
    return lax.ppermute(value, axis, [(i, (i + by) % size) for i in range(size)])


def tie(*values):
    return lax.optimization_barrier(values)


def body(activations, token_scales, out_grad, weight, logits, gumbel):
    y, zl, x = lax.axis_index("y"), lax.axis_index("zl"), lax.axis_index("x")
    zh, core = lax.axis_index("zh"), lax.axis_index("c")
    rows, features = activations.shape
    depth, hidden = weight.shape
    wide = 4 * depth

    blocks = out_grad.reshape(4, 2, 2, rows, hidden)
    blocks = jnp.where(core == 0, blocks, blocks[:, :, ::-1])
    blocks = jnp.where(zh == 0, blocks, blocks[:, ::-1])
    blocks = jnp.concatenate(
        [lax.dynamic_slice_in_dim(blocks, (x - j) % 4, 1, 0) for j in range(4)], axis=0
    )
    own = blocks.transpose(2, 0, 1, 3, 4).reshape(16 * rows, hidden)
    half = 8 * rows

    local = (activations.astype(F32) * token_scales[:, None]).astype(BF16)
    pieces = []
    for k in range(4):
        pieces.append(
            jnp.concatenate(
                [
                    lax.dynamic_slice_in_dim(
                        local, ((y + k) % 4) * wide + ((zl - m) % 4) * depth, depth, 1
                    )
                    for m in range(4)
                ],
                axis=1,
            )
        )
    scaled = jnp.stack([pieces[0]] + [shift(pieces[k], "y", k) for k in (1, 2, 3)], axis=0)
    scaled, first, second = tie(scaled, own[:half], own[half:])
    chances, mask_full = soft_mask(logits, gumbel)
    weight_wide = weight.astype(F32)
    masked = (weight_wide * mask_full).astype(BF16)

    below_a, above_b = shift(first, "y", 1), shift(second, "y", -1)
    other = shift(scaled, "zh", 1)
    scaled, first, second, below_a, above_b, masked = tie(
        jnp.stack([scaled, other], axis=0), first, second, below_a, above_b, masked
    )

    below_b, above_a = shift(second, "y", 1), shift(first, "y", -1)
    masked_1 = shift(masked, "zl", 1)
    scaled_1, scaled_3 = shift(scaled, "x", 1), shift(scaled, "x", 3)
    below_b, above_a, masked_1, scaled, scaled_1, scaled_3, below_a, above_b = tie(
        below_b, above_a, masked_1, scaled, scaled_1, scaled_3, below_a, above_b
    )

    far_a, far_b = shift(below_a, "y", 1), shift(above_b, "y", -1)
    masked_2 = shift(masked_1, "zl", 1)
    scaled_2 = shift(scaled, "x", 2)
    near = jnp.stack([scaled, scaled_1, scaled_3], axis=0)
    near_core = shift(near, "c", 1)
    far_a, far_b, masked_2, scaled_2, near_core = tie(far_a, far_b, masked_2, scaled_2, near_core)

    masked_3 = shift(masked_2, "zl", 1)
    far_core = shift(scaled_2, "c", 1)
    scaled = jnp.concatenate(
        [near[:2], scaled_2[None], near[2:], near_core[:2], far_core[None], near_core[2:]], axis=0
    )
    scaled = scaled.transpose(2, 0, 1, 3, 4).reshape(4 * 16 * rows, wide)
    grads = jnp.concatenate(
        [first, second, below_a, below_b, far_a, far_b, above_a, above_b], axis=0
    )

    grad_w = lax.dot_general(
        scaled, grads, (((0,), (0,)), ((), ())), preferred_element_type=F32
    ).reshape(4, depth, hidden)
    moving = grad_w[1].astype(BF16)
    masked_wide = jnp.concatenate([masked, masked_1, masked_2, masked_3], axis=0)

    grads = grads.reshape(4, 2, 4, 2 * rows, hidden)
    given = lax.dot_general(
        grads[:, 1], masked_wide, (((3,), (1,)), ((), ())), preferred_element_type=F32
    ).astype(BF16)

    given = shift(given, "c", 1)
    kept = lax.dot_general(
        grads[:, 0], masked_wide, (((3,), (1,)), ((), ())), preferred_element_type=F32
    )
    total = kept + given.astype(F32)
    sent = total.astype(BF16)
    moving = (shift(moving, "zl", 1).astype(F32) + grad_w[2]).astype(BF16)
    total, sent, moving = tie(total[:, 0], sent, moving)

    moving = (shift(moving, "zl", 1).astype(F32) + grad_w[3]).astype(BF16)
    sent_1, sent_3 = shift(sent[:, 1], "x", -1), shift(sent[:, 3], "x", -3)
    moving, sent_1, sent_3, sent_2 = tie(moving, sent_1, sent_3, sent[:, 2])

    moving = shift(moving, "zl", 1)
    sent_2 = shift(sent_2, "x", 2)
    total = total + sent_1.astype(F32) + sent_2.astype(F32) + sent_3.astype(F32)
    total, moving = tie(total, moving)

    total = total.reshape(4, 2, rows, wide)
    total = total[:, 0] + shift(total[:, 1].astype(BF16), "zh", 1).astype(F32)
    total = total.astype(BF16)
    parts = [total[0]] + [shift(total[k], "y", -k) for k in (1, 2, 3)]
    parts = jnp.stack(parts, axis=1)
    parts = jnp.concatenate(
        [lax.dynamic_slice_in_dim(parts, (q - y) % 4, 1, 1) for q in range(4)], axis=1
    ).reshape(rows, 4, 4, depth)
    parts = jnp.concatenate(
        [lax.dynamic_slice_in_dim(parts, (zl - q) % 4, 1, 2) for q in range(4)], axis=2
    )
    input_grad = parts.reshape(rows, features)

    return (input_grad, logit_grads(chances, (moving.astype(F32) + grad_w[0]) * weight_wide))


def solution(mesh):
    fine = Mesh(mesh.devices.reshape(4, 4, 4, 2, 2), ("y", "zl", "x", "zh", "c"))
    dp, tensor = ("y", "zl"), ("x", "zh", "c")
    return jax.shard_map(
        body,
        mesh=fine,
        in_specs=(
            P(dp + tensor, None),
            P(dp + tensor),
            P(dp, tensor),
            P(dp, tensor),
            P(None, dp, tensor),
            P(None, dp, tensor),
        ),
        out_specs=(P(dp + tensor, None), P(None, dp, tensor)),
        check_vma=False,
    )
```

```python
import jax
import jax.numpy as jnp
from jax import lax
from jax.sharding import Mesh, PartitionSpec as P

PATTERN_PAIRS = ((0, 1), (0, 2), (0, 3), (1, 2), (1, 3), (2, 3))
inverse_temp = 0.5
F32, BF16 = jnp.float32, jnp.bfloat16


def soft_mask(logits, gumbel):
    exponent = jnp.exp((logits + gumbel) * inverse_temp)
    chances = exponent / jnp.sum(exponent, axis=0)
    kept_slots = []
    for position in range(4):
        chosen = [chances[which] for which in range(6) if position in PATTERN_PAIRS[which]]
        kept_slots.append(chosen[0] + chosen[1] + chosen[2])
    mask_full = jnp.stack(kept_slots, axis=1)
    return (chances, mask_full.reshape(-1, mask_full.shape[2]))


def logit_grads(chances, mask_grad):
    groups = mask_grad.reshape(-1, 4, mask_grad.shape[1])
    pattern = jnp.stack(
        [
            groups[:, first_slot] + groups[:, second_slot]
            for first_slot, second_slot in PATTERN_PAIRS
        ],
        axis=0,
    )
    average = jnp.sum(chances * pattern, axis=0)
    return chances * (pattern - average) * inverse_temp


def shift(value, axis, by):
    size = lax.axis_size(axis)
    return lax.ppermute(value, axis, [(i, (i + by) % size) for i in range(size)])


def tie(*values):
    return lax.optimization_barrier(values)


def in_place(parts, which):
    which = which.reshape((-1,) + (1,) * parts[0].ndim)
    placed = parts[0][None]
    for k in range(1, len(parts)):
        placed = jnp.where(which == k, parts[k][None], placed)
    return placed


def body(activations, token_scales, out_grad, weight, logits, gumbel):
    y, zl, x = lax.axis_index("y"), lax.axis_index("zl"), lax.axis_index("x")
    zh, core = lax.axis_index("zh"), lax.axis_index("c")
    rows, features = activations.shape
    depth, hidden = weight.shape
    wide = 4 * depth

    grads = lax.all_gather(out_grad, "y", axis=0, tiled=True)

    local = (activations.astype(F32) * token_scales[:, None]).astype(BF16)
    pieces = []
    for k in range(4):
        pieces.append(
            jnp.concatenate(
                [
                    lax.dynamic_slice_in_dim(
                        local, ((y + k) % 4) * wide + ((zl + m) % 4) * depth, depth, 1
                    )
                    for m in range(4)
                ],
                axis=1,
            )
        )
    pieces = [pieces[0]] + [shift(pieces[k], "y", k) for k in (1, 2, 3)]
    scaled = in_place(pieces, (y - jnp.arange(4)) % 4)

    chances, mask_full = soft_mask(logits, gumbel)
    weight_wide = weight.astype(F32)
    masked = (weight_wide * mask_full).astype(BF16)

    other = shift(scaled, "zh", 1)
    masked_1 = shift(masked, "zl", -1)
    near = [scaled] + [shift(scaled, "x", j) for j in (1, 2, 3)]
    other, masked_1, *near = tie(other, masked_1, *near)

    masked_2 = shift(masked_1, "zl", -1)
    far = [other] + [shift(other, "x", j) for j in (1, 2, 3)]
    near_core = shift(jnp.stack(near, axis=0), "c", 1)
    masked_2, near_core, *far = tie(masked_2, near_core, *far)

    masked_3 = shift(masked_2, "zl", -1)
    far_core = shift(jnp.stack(far, axis=0), "c", 1)
    scaled = jnp.zeros((4, 4, 2, 2, rows, wide), BF16)
    for parts, on_zh, on_core in (
        (near, zh, core),
        (near_core, zh, 1 - core),
        (far, 1 - zh, core),
        (far_core, 1 - zh, 1 - core),
    ):
        for j in range(4):
            scaled = lax.dynamic_update_slice(
                scaled, parts[j][:, None, None, None], (0, (x - j) % 4, on_zh, on_core, 0, 0)
            )
    scaled = scaled.reshape(4 * 16 * rows, wide)

    grad_w = lax.dot_general(
        scaled, grads, (((0,), (0,)), ((), ())), preferred_element_type=F32
    ).reshape(4, depth, hidden)
    moving = grad_w[1].astype(BF16)

    grads = grads.reshape(32, 2, rows, hidden)
    mine = lax.dynamic_index_in_dim(grads, core, 1, False).reshape(32 * rows, hidden)
    its = lax.dynamic_index_in_dim(grads, 1 - core, 1, False).reshape(32 * rows, hidden)
    sent, totals = [], []
    for pair in ((masked, masked_1), (masked_2, masked_3)):
        pair = jnp.concatenate(pair, axis=0)
        given = lax.dot_general(
            its, pair, (((1,), (1,)), ((), ())), preferred_element_type=F32
        ).astype(BF16)
        given = shift(given, "c", 1)
        kept = lax.dot_general(
            mine, pair, (((1,), (1,)), ((), ())), preferred_element_type=F32
        )
        total = (kept + given.astype(F32)).reshape(4, 4, 2 * rows, 2 * depth)
        totals.append(lax.dynamic_index_in_dim(total, x, 1, False))
        total = total.astype(BF16)
        sent.append([lax.dynamic_index_in_dim(total, (x - j) % 4, 1, False) for j in (1, 2, 3)])

    moving = (shift(moving, "zl", -1).astype(F32) + grad_w[2]).astype(BF16)
    first = [shift(sent[0][j - 1], "x", -j) for j in (1, 2, 3)]
    out = tie(moving, *first, *sent[1])
    moving, first, second = out[0], out[1:4], out[4:]

    moving = (shift(moving, "zl", -1).astype(F32) + grad_w[3]).astype(BF16)
    second = [shift(second[j - 1], "x", -j) for j in (1, 2, 3)]
    moving, *second = tie(moving, *second)

    total = jnp.concatenate(
        [
            base + parts[0].astype(F32) + parts[1].astype(F32) + parts[2].astype(F32)
            for base, parts in zip(totals, (first, second))
        ],
        axis=-1,
    ).reshape(4, 2, rows, wide)
    moving = shift(moving, "zl", -1)
    other = shift(lax.dynamic_index_in_dim(total, 1 - zh, 1, False).astype(BF16), "zh", 1)
    other, moving = tie(other, moving)

    total = lax.dynamic_index_in_dim(total, zh, 1, False) + other.astype(F32)
    total = total.astype(BF16)
    total = jnp.concatenate([total, total], axis=2)
    total = lax.dynamic_slice_in_dim(total, ((4 - zl) % 4) * depth, wide, 2)
    parts = [lax.dynamic_index_in_dim(total, (y - k) % 4, 0, False) for k in range(4)]
    parts = [parts[0]] + [shift(parts[k], "y", -k) for k in (1, 2, 3)]
    parts = in_place(parts, (jnp.arange(4) - y) % 4)
    input_grad = parts.transpose(1, 0, 2).reshape(rows, features)

    return (input_grad, logit_grads(chances, (moving.astype(F32) + grad_w[0]) * weight_wide))


def solution(mesh):
    fine = Mesh(mesh.devices.reshape(4, 4, 4, 2, 2), ("y", "zl", "x", "zh", "c"))
    dp, tensor = ("y", "zl"), ("x", "zh", "c")
    return jax.shard_map(
        body,
        mesh=fine,
        in_specs=(
            P(dp + tensor, None),
            P(dp + tensor),
            P(dp, tensor),
            P(dp, tensor),
            P(None, dp, tensor),
            P(None, dp, tensor),
        ),
        out_specs=(P(dp + tensor, None), P(None, dp, tensor)),
        check_vma=False,
    )
```

```python
import jax
import jax.numpy as jnp
from jax import lax
from jax.sharding import Mesh, PartitionSpec as P

PATTERN_PAIRS = ((0, 1), (0, 2), (0, 3), (1, 2), (1, 3), (2, 3))
inverse_temp = 0.5
F32, BF16 = jnp.float32, jnp.bfloat16


def soft_mask(logits, gumbel):
    exponent = jnp.exp((logits + gumbel) * inverse_temp)
    chances = exponent / jnp.sum(exponent, axis=0)
    kept_slots = []
    for position in range(4):
        chosen = [chances[which] for which in range(6) if position in PATTERN_PAIRS[which]]
        kept_slots.append(chosen[0] + chosen[1] + chosen[2])
    mask_full = jnp.stack(kept_slots, axis=1)
    return (chances, mask_full.reshape(-1, mask_full.shape[2]))


def logit_grads(chances, mask_grad):
    groups = mask_grad.reshape(-1, 4, mask_grad.shape[1])
    pattern = jnp.stack(
        [
            groups[:, first_slot] + groups[:, second_slot]
            for first_slot, second_slot in PATTERN_PAIRS
        ],
        axis=0,
    )
    average = jnp.sum(chances * pattern, axis=0)
    return chances * (pattern - average) * inverse_temp


def shift(value, axis, by):
    size = lax.axis_size(axis)
    return lax.ppermute(value, axis, [(i, (i + by) % size) for i in range(size)])


def tie(*values):
    return lax.optimization_barrier(values)


def in_place(parts, which):
    which = which.reshape((-1,) + (1,) * parts[0].ndim)
    placed = parts[0][None]
    for k in range(1, len(parts)):
        placed = jnp.where(which == k, parts[k][None], placed)
    return placed


def body(activations, token_scales, out_grad, weight, logits, gumbel):
    y, zl, x = lax.axis_index("y"), lax.axis_index("zl"), lax.axis_index("x")
    zh, core = lax.axis_index("zh"), lax.axis_index("c")
    rows, features = activations.shape
    depth, hidden = weight.shape
    wide = 4 * depth

    own = out_grad.reshape(8, 2, rows, hidden).transpose(1, 0, 2, 3).reshape(16 * rows, hidden)
    half = 8 * rows

    local = (activations.astype(F32) * token_scales[:, None]).astype(BF16)
    pieces = []
    for k in range(4):
        pieces.append(
            jnp.concatenate(
                [
                    lax.dynamic_slice_in_dim(
                        local, ((y + k) % 4) * wide + ((zl + m) % 4) * depth, depth, 1
                    )
                    for m in range(4)
                ],
                axis=1,
            )
        )
    scaled = jnp.stack([pieces[0]] + [shift(pieces[k], "y", k) for k in (1, 2, 3)], axis=0)
    scaled, own = tie(scaled, own)

    chances, mask_full = soft_mask(logits, gumbel)
    weight_wide = weight.astype(F32)
    masked = (weight_wide * mask_full).astype(BF16)

    other = shift(scaled, "zh", 1)
    masked_1 = shift(masked, "zl", -1)
    below, above = shift(own, "y", 1), shift(own, "y", -1)
    other, masked_1, below, above = tie(other, masked_1, below, above)
    scaled = in_place([scaled, other], jnp.where(zh == 0, jnp.arange(2), 1 - jnp.arange(2)))

    masked_2 = shift(masked_1, "zl", -1)
    far_a, far_b = shift(below[:half], "y", 1), shift(above[half:], "y", -1)
    scaled_1, scaled_3 = shift(scaled, "x", 1), shift(scaled, "x", 3)
    masked_2, far_a, far_b, scaled, scaled_1, scaled_3 = tie(
        masked_2, far_a, far_b, scaled, scaled_1, scaled_3
    )
    grads = jnp.concatenate([own, below, far_a, far_b, above], axis=0)

    masked_3 = shift(masked_2, "zl", -1)
    scaled_2 = shift(scaled, "x", 2)
    near = (scaled, scaled_1, scaled_3)
    near_core = shift(jnp.stack(near, axis=0), "c", 1)
    scaled_2, near_core = tie(scaled_2, near_core)
    far_core = shift(scaled_2, "c", 1)
    rows_of = jnp.zeros((4, 2, 4, 2, rows, wide), BF16)
    for part, j, on_core in (
        (near[0], 0, core),
        (near[1], 1, core),
        (near[2], 3, core),
        (near_core[0], 0, 1 - core),
        (near_core[1], 1, 1 - core),
        (near_core[2], 3, 1 - core),
        (scaled_2, 2, core),
        (far_core, 2, 1 - core),
    ):
        part = part.transpose(1, 0, 2, 3)[:, None, None]
        rows_of = lax.dynamic_update_slice(rows_of, part, (0, on_core, (x - j) % 4, 0, 0, 0))
    scaled = rows_of.reshape(4 * 16 * rows, wide)

    grad_w = [
        lax.dot_general(
            scaled[:, m * depth : (m + 1) * depth],
            grads,
            (((0,), (0,)), ((), ())),
            preferred_element_type=F32,
        )
        for m in range(4)
    ]
    moving = grad_w[1].astype(BF16)

    grads = grads.reshape(4, 2, half, hidden)
    mine = lax.dynamic_index_in_dim(grads, core, 1, False).reshape(4 * half, hidden)
    its = lax.dynamic_index_in_dim(grads, 1 - core, 1, False).reshape(4 * half, hidden)
    sent, totals = [], []
    for pair in ((masked, masked_1), (masked_2, masked_3)):
        pair = jnp.concatenate(pair, axis=0)
        given = lax.dot_general(
            its, pair, (((1,), (1,)), ((), ())), preferred_element_type=F32
        ).astype(BF16)
        given = shift(given, "c", 1)
        kept = lax.dot_general(
            mine, pair, (((1,), (1,)), ((), ())), preferred_element_type=F32
        )
        total = (kept + given.astype(F32)).reshape(4, 4, 2 * rows, 2 * depth)
        totals.append(lax.dynamic_index_in_dim(total, x, 1, False))
        total = total.astype(BF16)
        sent.append([lax.dynamic_index_in_dim(total, (x - j) % 4, 1, False) for j in (1, 2, 3)])

    moving = (shift(moving, "zl", -1).astype(F32) + grad_w[2]).astype(BF16)

    moving = (shift(moving, "zl", -1).astype(F32) + grad_w[3]).astype(BF16)
    first = [shift(sent[0][j - 1], "x", -j) for j in (1, 2, 3)]
    out = tie(moving, *first, *sent[1])
    moving, first, second = out[0], out[1:4], out[4:]

    moving = shift(moving, "zl", -1)
    second = [shift(second[j - 1], "x", -j) for j in (1, 2, 3)]
    moving, *second = tie(moving, *second)

    total = jnp.concatenate(
        [
            base + parts[0].astype(F32) + parts[1].astype(F32) + parts[2].astype(F32)
            for base, parts in zip(totals, (first, second))
        ],
        axis=-1,
    ).reshape(4, 2, rows, wide)
    other = shift(lax.dynamic_index_in_dim(total, 1 - zh, 1, False).astype(BF16), "zh", 1)

    total = lax.dynamic_index_in_dim(total, zh, 1, False) + other.astype(F32)
    total = total.astype(BF16)
    total = jnp.concatenate([total, total], axis=2)
    total = lax.dynamic_slice_in_dim(total, ((4 - zl) % 4) * depth, wide, 2)
    parts = [total[0]] + [shift(total[k], "y", -k) for k in (1, 2, 3)]
    parts = jnp.concatenate(parts + parts, axis=1)
    input_grad = lax.dynamic_slice_in_dim(parts, ((4 - y) % 4) * wide, features, 1)

    return (input_grad, logit_grads(chances, (moving.astype(F32) + grad_w[0]) * weight_wide))


def solution(mesh):
    fine = Mesh(mesh.devices.reshape(4, 4, 4, 2, 2), ("y", "zl", "x", "zh", "c"))
    dp, tensor = ("y", "zl"), ("x", "zh", "c")
    return jax.shard_map(
        body,
        mesh=fine,
        in_specs=(
            P(dp + tensor, None),
            P(dp + tensor),
            P(dp, tensor),
            P(dp, tensor),
            P(None, dp, tensor),
            P(None, dp, tensor),
        ),
        out_specs=(P(dp + tensor, None), P(None, dp, tensor)),
        check_vma=False,
    )
```

```python
import jax
import jax.numpy as jnp
from jax import lax
from jax.sharding import Mesh, PartitionSpec as P

PATTERN_PAIRS = ((0, 1), (0, 2), (0, 3), (1, 2), (1, 3), (2, 3))
inverse_temp = 0.5
F32, BF16 = jnp.float32, jnp.bfloat16


def soft_mask(logits, gumbel):
    exponent = jnp.exp((logits + gumbel) * inverse_temp)
    chances = exponent / jnp.sum(exponent, axis=0)
    kept_slots = []
    for position in range(4):
        chosen = [chances[which] for which in range(6) if position in PATTERN_PAIRS[which]]
        kept_slots.append(chosen[0] + chosen[1] + chosen[2])
    mask_full = jnp.stack(kept_slots, axis=1)
    return (chances, mask_full.reshape(-1, mask_full.shape[2]))


def logit_grads(chances, mask_grad):
    groups = mask_grad.reshape(-1, 4, mask_grad.shape[1])
    pattern = jnp.stack(
        [
            groups[:, first_slot] + groups[:, second_slot]
            for first_slot, second_slot in PATTERN_PAIRS
        ],
        axis=0,
    )
    average = jnp.sum(chances * pattern, axis=0)
    return chances * (pattern - average) * inverse_temp


def shift(value, axis, by):
    size = lax.axis_size(axis)
    return lax.ppermute(value, axis, [(i, (i + by) % size) for i in range(size)])


def tie(*values):
    return lax.optimization_barrier(values)


def in_place(parts, which):
    which = which.reshape((-1,) + (1,) * parts[0].ndim)
    placed = parts[0][None]
    for k in range(1, len(parts)):
        placed = jnp.where(which == k, parts[k][None], placed)
    return placed


def body(activations, token_scales, out_grad, weight, logits, gumbel):
    y, zl, x = lax.axis_index("y"), lax.axis_index("zl"), lax.axis_index("x")
    zh, core = lax.axis_index("zh"), lax.axis_index("c")
    rows, features = activations.shape
    depth, hidden = weight.shape
    wide = 4 * depth

    own = out_grad.reshape(8, 2, rows, hidden).transpose(1, 0, 2, 3).reshape(16 * rows, hidden)
    half = 8 * rows

    local = (activations.astype(F32) * token_scales[:, None]).astype(BF16)
    pieces = []
    for k in range(4):
        pieces.append(
            jnp.concatenate(
                [
                    lax.dynamic_slice_in_dim(
                        local, ((y + k) % 4) * wide + ((zl + m) % 4) * depth, depth, 1
                    )
                    for m in range(4)
                ],
                axis=1,
            )
        )
    scaled = jnp.stack([pieces[0]] + [shift(pieces[k], "y", k) for k in (1, 2, 3)], axis=0)
    scaled, own = tie(scaled, own)

    chances, mask_full = soft_mask(logits, gumbel)
    weight_wide = weight.astype(F32)
    masked = (weight_wide * mask_full).astype(BF16)

    other = shift(scaled, "zh", 1)
    other, masked = tie(other, masked)
    scaled = in_place([scaled, other], jnp.where(zh == 0, jnp.arange(2), 1 - jnp.arange(2)))

    masked_1 = shift(masked, "zl", -1)
    below, above = shift(own, "y", 1), shift(own, "y", -1)
    scaled_1, scaled_3 = shift(scaled, "x", 1), shift(scaled, "x", 3)
    masked_1, below, above, scaled, scaled_1, scaled_3 = tie(
        masked_1, below, above, scaled, scaled_1, scaled_3
    )

    masked_2 = shift(masked_1, "zl", -1)
    far_a, far_b = shift(below[:half], "y", 1), shift(above[half:], "y", -1)
    scaled_2 = shift(scaled, "x", 2)
    near = (scaled, scaled_1, scaled_3)
    near_core = shift(jnp.stack(near, axis=0), "c", 1)
    masked_2, far_a, far_b, scaled_2, near_core = tie(
        masked_2, far_a, far_b, scaled_2, near_core
    )
    grads = jnp.concatenate([own, below, far_a, far_b, above], axis=0)

    masked_3 = shift(masked_2, "zl", -1)
    far_core = shift(scaled_2, "c", 1)
    rows_of = jnp.zeros((4, 2, 4, 2, rows, wide), BF16)
    for part, j, on_core in (
        (near[0], 0, core),
        (near[1], 1, core),
        (near[2], 3, core),
        (near_core[0], 0, 1 - core),
        (near_core[1], 1, 1 - core),
        (near_core[2], 3, 1 - core),
        (scaled_2, 2, core),
        (far_core, 2, 1 - core),
    ):
        part = part.transpose(1, 0, 2, 3)[:, None, None]
        rows_of = lax.dynamic_update_slice(rows_of, part, (0, on_core, (x - j) % 4, 0, 0, 0))
    scaled = rows_of.reshape(4 * 16 * rows, wide)

    grad_w = [
        lax.dot_general(
            scaled[:, m * depth : (m + 1) * depth],
            grads,
            (((0,), (0,)), ((), ())),
            preferred_element_type=F32,
        )
        for m in range(4)
    ]
    moving = grad_w[1].astype(BF16)

    grads = grads.reshape(4, 2, half, hidden)
    mine = lax.dynamic_index_in_dim(grads, core, 1, False).reshape(4 * half, hidden)
    its = lax.dynamic_index_in_dim(grads, 1 - core, 1, False).reshape(4 * half, hidden)
    sent, totals = [], []
    for pair in ((masked, masked_1), (masked_2, masked_3)):
        pair = jnp.concatenate(pair, axis=0)
        given = lax.dot_general(
            its, pair, (((1,), (1,)), ((), ())), preferred_element_type=F32
        ).astype(BF16)
        given = shift(given, "c", 1)
        kept = lax.dot_general(
            mine, pair, (((1,), (1,)), ((), ())), preferred_element_type=F32
        )
        total = (kept + given.astype(F32)).reshape(4, 4, 2 * rows, 2 * depth)
        totals.append(lax.dynamic_index_in_dim(total, x, 1, False))
        total = total.astype(BF16)
        sent.append([lax.dynamic_index_in_dim(total, (x - j) % 4, 1, False) for j in (1, 2, 3)])

    moving = shift(moving, "zl", -1)
    first = [shift(sent[0][j - 1], "x", -j) for j in (1, 2, 3)]
    out = tie(moving, *first, *sent[1])
    moving, first, second = out[0], out[1:4], out[4:]
    moving = (moving.astype(F32) + grad_w[2]).astype(BF16)

    moving = shift(moving, "zl", -1)
    second = [shift(second[j - 1], "x", -j) for j in (1, 2, 3)]
    moving, *second = tie(moving, *second)
    moving = (moving.astype(F32) + grad_w[3]).astype(BF16)

    total = jnp.concatenate(
        [
            base + parts[0].astype(F32) + parts[1].astype(F32) + parts[2].astype(F32)
            for base, parts in zip(totals, (first, second))
        ],
        axis=-1,
    ).reshape(4, 2, rows, wide)
    other = shift(lax.dynamic_index_in_dim(total, 1 - zh, 1, False).astype(BF16), "zh", 1)
    moving = shift(moving, "zl", -1)
    other, moving = tie(other, moving)

    total = lax.dynamic_index_in_dim(total, zh, 1, False) + other.astype(F32)
    total = total.astype(BF16)
    total = jnp.concatenate([total, total], axis=2)
    total = lax.dynamic_slice_in_dim(total, ((4 - zl) % 4) * depth, wide, 2)
    parts = [total[0]] + [shift(total[k], "y", -k) for k in (1, 2, 3)]
    parts = jnp.concatenate(parts + parts, axis=1)
    input_grad = lax.dynamic_slice_in_dim(parts, ((4 - y) % 4) * wide, features, 1)

    return (input_grad, logit_grads(chances, (moving.astype(F32) + grad_w[0]) * weight_wide))


def solution(mesh):
    fine = Mesh(mesh.devices.reshape(4, 4, 4, 2, 2), ("y", "zl", "x", "zh", "c"))
    dp, tensor = ("y", "zl"), ("x", "zh", "c")
    return jax.shard_map(
        body,
        mesh=fine,
        in_specs=(
            P(dp + tensor, None),
            P(dp + tensor),
            P(dp, tensor),
            P(dp, tensor),
            P(None, dp, tensor),
            P(None, dp, tensor),
        ),
        out_specs=(P(dp + tensor, None), P(None, dp, tensor)),
        check_vma=False,
    )
```

```python
import jax
import jax.numpy as jnp
from jax import lax
from jax.sharding import Mesh, PartitionSpec as P

PATTERN_PAIRS = ((0, 1), (0, 2), (0, 3), (1, 2), (1, 3), (2, 3))
inverse_temp = 0.5
F32, BF16 = jnp.float32, jnp.bfloat16


def soft_mask(logits, gumbel):
    exponent = jnp.exp((logits + gumbel) * inverse_temp)
    chances = exponent / jnp.sum(exponent, axis=0)
    kept_slots = []
    for position in range(4):
        chosen = [chances[which] for which in range(6) if position in PATTERN_PAIRS[which]]
        kept_slots.append(chosen[0] + chosen[1] + chosen[2])
    mask_full = jnp.stack(kept_slots, axis=1)
    return (chances, mask_full.reshape(-1, mask_full.shape[2]))


def logit_grads(chances, mask_grad):
    groups = mask_grad.reshape(-1, 4, mask_grad.shape[1])
    pattern = jnp.stack(
        [
            groups[:, first_slot] + groups[:, second_slot]
            for first_slot, second_slot in PATTERN_PAIRS
        ],
        axis=0,
    )
    average = jnp.sum(chances * pattern, axis=0)
    return chances * (pattern - average) * inverse_temp


def shift(value, axis, by):
    size = lax.axis_size(axis)
    return lax.ppermute(value, axis, [(i, (i + by) % size) for i in range(size)])


def tie(*values):
    return lax.optimization_barrier(values)


def in_place(parts, which):
    which = which.reshape((-1,) + (1,) * parts[0].ndim)
    placed = parts[0][None]
    for k in range(1, len(parts)):
        placed = jnp.where(which == k, parts[k][None], placed)
    return placed


def body(activations, token_scales, out_grad, weight, logits, gumbel):
    y, zl, x = lax.axis_index("y"), lax.axis_index("zl"), lax.axis_index("x")
    zh, core = lax.axis_index("zh"), lax.axis_index("c")
    rows, features = activations.shape
    depth, hidden = weight.shape
    wide = 4 * depth

    own = out_grad.reshape(8, 2, rows, hidden).transpose(1, 0, 2, 3).reshape(16 * rows, hidden)
    half = 8 * rows

    local = (activations.astype(F32) * token_scales[:, None]).astype(BF16)
    local = jnp.stack(
        [
            jnp.concatenate(
                [
                    lax.dynamic_slice_in_dim(
                        local, k * wide + ((zl + m) % 4) * depth, depth, 1
                    )
                    for m in range(4)
                ],
                axis=1,
            )
            for k in range(4)
        ],
        axis=0,
    )

    other = shift(local, "zh", 1)
    chances, mask_full = soft_mask(logits, gumbel)
    weight_wide = weight.astype(F32)
    masked = (weight_wide * mask_full).astype(BF16)
    other, masked, own = tie(other, masked, own)
    local = jnp.concatenate(
        [jnp.where(zh == 0, local, other), jnp.where(zh == 0, other, local)], axis=1
    )

    masked_1 = shift(masked, "zl", -1)
    below, above = shift(own, "y", 1), shift(own, "y", -1)
    scaled = lax.all_to_all(local, "y", 0, 0, tiled=True)
    masked_1, scaled = tie(masked_1, scaled)
    scaled = in_place([scaled[k] for k in range(4)], (y - jnp.arange(4)) % 4)

    masked_2 = shift(masked_1, "zl", -1)
    scaled_1, scaled_3 = shift(scaled, "x", 1), shift(scaled, "x", 3)
    masked_2, below, above, scaled, scaled_1, scaled_3 = tie(
        masked_2, below, above, scaled, scaled_1, scaled_3
    )

    masked_3 = shift(masked_2, "zl", -1)
    far_a, far_b = shift(below[:half], "y", 1), shift(above[half:], "y", -1)
    scaled_2 = shift(scaled, "x", 2)
    near = (scaled, scaled_1, scaled_3)
    near_core = shift(jnp.stack(near, axis=0), "c", 1)
    masked_3, far_a, far_b, scaled_2, near_core = tie(
        masked_3, far_a, far_b, scaled_2, near_core
    )
    grads = jnp.concatenate([own, below, far_a, far_b, above], axis=0)

    far_core = shift(scaled_2, "c", 1)
    rows_of = jnp.zeros((4, 2, 4, 2 * rows, wide), BF16)
    for part, j, on_core in (
        (near[0], 0, core),
        (near[1], 1, core),
        (near[2], 3, core),
        (near_core[0], 0, 1 - core),
        (near_core[1], 1, 1 - core),
        (near_core[2], 3, 1 - core),
        (scaled_2, 2, core),
        (far_core, 2, 1 - core),
    ):
        part = part[:, None, None]
        rows_of = lax.dynamic_update_slice(rows_of, part, (0, on_core, (x - j) % 4, 0, 0))
    scaled = rows_of.reshape(4 * 16 * rows, wide)

    grad_w = [
        lax.dot_general(
            scaled[:, m * depth : (m + 1) * depth],
            grads,
            (((0,), (0,)), ((), ())),
            preferred_element_type=F32,
        )
        for m in range(4)
    ]
    moving = grad_w[1].astype(BF16)

    grads = grads.reshape(4, 2, half, hidden)
    mine = lax.dynamic_index_in_dim(grads, core, 1, False).reshape(4 * half, hidden)
    its = lax.dynamic_index_in_dim(grads, 1 - core, 1, False).reshape(4 * half, hidden)
    sent, totals = [], []
    for pair in ((masked, masked_1), (masked_2, masked_3)):
        pair = jnp.concatenate(pair, axis=0)
        given = lax.dot_general(
            its, pair, (((1,), (1,)), ((), ())), preferred_element_type=F32
        ).astype(BF16)
        given = shift(given, "c", 1)
        kept = lax.dot_general(
            mine, pair, (((1,), (1,)), ((), ())), preferred_element_type=F32
        )
        total = (kept + given.astype(F32)).reshape(4, 4, 2 * rows, 2 * depth)
        totals.append(lax.dynamic_index_in_dim(total, x, 1, False))
        total = total.astype(BF16)
        sent.append([lax.dynamic_index_in_dim(total, (x - j) % 4, 1, False) for j in (1, 2, 3)])

    for m in (2, 3):
        moving = (shift(moving, "zl", -1).astype(F32) + grad_w[m]).astype(BF16)
    moving = shift(moving, "zl", -1)

    first = [shift(sent[0][j - 1], "x", -j) for j in (1, 2, 3)]
    out = tie(*first, *sent[1])
    first, second = out[:3], out[3:]
    second = [shift(second[j - 1], "x", -j) for j in (1, 2, 3)]

    total = jnp.concatenate(
        [
            base + parts[0].astype(F32) + parts[1].astype(F32) + parts[2].astype(F32)
            for base, parts in zip(totals, (first, second))
        ],
        axis=-1,
    ).reshape(4, 2, rows, wide)
    other = shift(lax.dynamic_index_in_dim(total, 1 - zh, 1, False).astype(BF16), "zh", 1)

    total = lax.dynamic_index_in_dim(total, zh, 1, False) + other.astype(F32)
    total = total.astype(BF16)
    total = jnp.concatenate([total, total], axis=2)
    total = lax.dynamic_slice_in_dim(total, ((4 - zl) % 4) * depth, wide, 2)
    parts = [total[0]] + [shift(total[k], "y", -k) for k in (1, 2, 3)]
    input_grad = jnp.zeros((rows, features), BF16)
    for k in range(4):
        input_grad = lax.dynamic_update_slice(input_grad, parts[k], (0, ((y + k) % 4) * wide))

    return (input_grad, logit_grads(chances, (moving.astype(F32) + grad_w[0]) * weight_wide))


def solution(mesh):
    fine = Mesh(mesh.devices.reshape(4, 4, 4, 2, 2), ("y", "zl", "x", "zh", "c"))
    dp, tensor = ("y", "zl"), ("x", "zh", "c")
    return jax.shard_map(
        body,
        mesh=fine,
        in_specs=(
            P(dp + tensor, None),
            P(dp + tensor),
            P(dp, tensor),
            P(dp, tensor),
            P(None, dp, tensor),
            P(None, dp, tensor),
        ),
        out_specs=(P(dp + tensor, None), P(None, dp, tensor)),
        check_vma=False,
    )
```

```python
import jax
import jax.numpy as jnp
from jax import lax
from jax.sharding import Mesh, PartitionSpec as P

PATTERN_PAIRS = ((0, 1), (0, 2), (0, 3), (1, 2), (1, 3), (2, 3))
inverse_temp = 0.5
F32, BF16 = jnp.float32, jnp.bfloat16


def soft_mask(logits, gumbel):
    exponent = jnp.exp((logits + gumbel) * inverse_temp)
    chances = exponent / jnp.sum(exponent, axis=0)
    kept_slots = []
    for position in range(4):
        chosen = [chances[which] for which in range(6) if position in PATTERN_PAIRS[which]]
        kept_slots.append(chosen[0] + chosen[1] + chosen[2])
    mask_full = jnp.stack(kept_slots, axis=1)
    return (chances, mask_full.reshape(-1, mask_full.shape[2]))


def logit_grads(chances, mask_grad):
    groups = mask_grad.reshape(-1, 4, mask_grad.shape[1])
    pattern = jnp.stack(
        [
            groups[:, first_slot] + groups[:, second_slot]
            for first_slot, second_slot in PATTERN_PAIRS
        ],
        axis=0,
    )
    average = jnp.sum(chances * pattern, axis=0)
    return chances * (pattern - average) * inverse_temp


def shift(value, axis, by):
    size = lax.axis_size(axis)
    return lax.ppermute(value, axis, [(i, (i + by) % size) for i in range(size)])


def tie(*values):
    return lax.optimization_barrier(values)


def in_place(parts, which):
    which = which.reshape((-1,) + (1,) * parts[0].ndim)
    placed = parts[0][None]
    for k in range(1, len(parts)):
        placed = jnp.where(which == k, parts[k][None], placed)
    return placed


def input_part(mine, its, masked, x):
    given = lax.dot_general(
        its, masked, (((1,), (1,)), ((), ())), preferred_element_type=F32
    ).astype(BF16)
    given = shift(given, "c", 1)
    kept = lax.dot_general(mine, masked, (((1,), (1,)), ((), ())), preferred_element_type=F32)
    total = (kept + given.astype(F32)).reshape(4, 4, mine.shape[0] // 16, masked.shape[0])
    base = lax.dynamic_index_in_dim(total, x, 1, False)
    total = total.astype(BF16)
    sent = [lax.dynamic_index_in_dim(total, (x - j) % 4, 1, False) for j in (1, 2, 3)]
    return base, *sent


def body(activations, token_scales, out_grad, weight, logits, gumbel):
    y, zl, x = lax.axis_index("y"), lax.axis_index("zl"), lax.axis_index("x")
    zh, core = lax.axis_index("zh"), lax.axis_index("c")
    rows, features = activations.shape
    depth, hidden = weight.shape
    wide = 4 * depth

    own = out_grad.reshape(8, 2, rows, hidden).transpose(1, 0, 2, 3).reshape(16 * rows, hidden)
    half = 8 * rows

    local = (activations.astype(F32) * token_scales[:, None]).astype(BF16)
    local = jnp.stack(
        [
            jnp.concatenate(
                [
                    lax.dynamic_slice_in_dim(
                        local, k * wide + ((zl + m) % 4) * depth, depth, 1
                    )
                    for m in range(4)
                ],
                axis=1,
            )
            for k in range(4)
        ],
        axis=0,
    )

    other = shift(local, "zh", 1)
    chances, mask_full = soft_mask(logits, gumbel)
    weight_wide = weight.astype(F32)
    masked = (weight_wide * mask_full).astype(BF16)
    other, masked = tie(other, masked)
    local = jnp.concatenate(
        [jnp.where(zh == 0, local, other), jnp.where(zh == 0, other, local)], axis=1
    )

    masked_1 = shift(masked, "zl", -1)
    below, above = shift(own, "y", 1), shift(own, "y", -1)
    scaled = lax.all_to_all(local, "y", 0, 0, tiled=True)
    masked_1, scaled, below, above = tie(masked_1, scaled, below, above)
    scaled = in_place([scaled[k] for k in range(4)], (y - jnp.arange(4)) % 4)

    masked_2 = shift(masked_1, "zl", -1)
    far_a, far_b = shift(below[:half], "y", 1), shift(above[half:], "y", -1)
    scaled_1, scaled_3 = shift(scaled, "x", 1), shift(scaled, "x", 3)
    pair = jnp.concatenate([masked, masked_1], axis=0)
    pair, masked_2, far_a, far_b, scaled, scaled_1, scaled_3 = tie(
        pair, masked_2, far_a, far_b, scaled, scaled_1, scaled_3
    )
    grads = jnp.concatenate([own, below, far_a, far_b, above], axis=0)
    halves = grads.reshape(4, 2, half, hidden)
    mine = lax.dynamic_index_in_dim(halves, core, 1, False).reshape(4 * half, hidden)
    its = lax.dynamic_index_in_dim(halves, 1 - core, 1, False).reshape(4 * half, hidden)

    masked_3 = shift(masked_2, "zl", -1)
    scaled_2 = shift(scaled, "x", 2)
    near = (scaled, scaled_1, scaled_3)
    near_core = shift(jnp.stack(near, axis=0), "c", 1)
    base_1, *first = input_part(mine, its, pair, x)
    masked_3, scaled_2, near_core, base_1, *first = tie(
        masked_3, scaled_2, near_core, base_1, *first
    )

    far_core = shift(scaled_2, "c", 1)
    first = [shift(first[j - 1], "x", -j) for j in (1, 2, 3)]
    pair = jnp.concatenate([masked_2, masked_3], axis=0)
    base_2, *second = input_part(mine, its, pair, x)
    out = tie(*first, *second)
    first, second = out[:3], out[3:]
    rows_of = jnp.zeros((4, 2, 4, 2 * rows, wide), BF16)
    for part, j, on_core in (
        (near[0], 0, core),
        (near[1], 1, core),
        (near[2], 3, core),
        (near_core[0], 0, 1 - core),
        (near_core[1], 1, 1 - core),
        (near_core[2], 3, 1 - core),
        (scaled_2, 2, core),
        (far_core, 2, 1 - core),
    ):
        part = part[:, None, None]
        rows_of = lax.dynamic_update_slice(rows_of, part, (0, on_core, (x - j) % 4, 0, 0))
    scaled = rows_of.reshape(4 * 16 * rows, wide)

    grad_w = [
        lax.dot_general(
            scaled[:, m * depth : (m + 1) * depth],
            grads,
            (((0,), (0,)), ((), ())),
            preferred_element_type=F32,
        )
        for m in range(4)
    ]
    moving = grad_w[1].astype(BF16)

    for m in (2, 3):
        moving = (shift(moving, "zl", -1).astype(F32) + grad_w[m]).astype(BF16)
    moving = shift(moving, "zl", -1)

    second = [shift(second[j - 1], "x", -j) for j in (1, 2, 3)]

    total = jnp.concatenate(
        [
            base + parts[0].astype(F32) + parts[1].astype(F32) + parts[2].astype(F32)
            for base, parts in ((base_1, first), (base_2, second))
        ],
        axis=-1,
    ).reshape(4, 2, rows, wide)
    other = shift(lax.dynamic_index_in_dim(total, 1 - zh, 1, False).astype(BF16), "zh", 1)

    total = lax.dynamic_index_in_dim(total, zh, 1, False) + other.astype(F32)
    total = total.astype(BF16)
    total = jnp.concatenate([total, total], axis=2)
    total = lax.dynamic_slice_in_dim(total, ((4 - zl) % 4) * depth, wide, 2)
    parts = [total[0]] + [shift(total[k], "y", -k) for k in (1, 2, 3)]
    input_grad = jnp.zeros((rows, features), BF16)
    for k in range(4):
        input_grad = lax.dynamic_update_slice(input_grad, parts[k], (0, ((y + k) % 4) * wide))

    return (input_grad, logit_grads(chances, (moving.astype(F32) + grad_w[0]) * weight_wide))


def solution(mesh):
    fine = Mesh(mesh.devices.reshape(4, 4, 4, 2, 2), ("y", "zl", "x", "zh", "c"))
    dp, tensor = ("y", "zl"), ("x", "zh", "c")
    return jax.shard_map(
        body,
        mesh=fine,
        in_specs=(
            P(dp + tensor, None),
            P(dp + tensor),
            P(dp, tensor),
            P(dp, tensor),
            P(None, dp, tensor),
            P(None, dp, tensor),
        ),
        out_specs=(P(dp + tensor, None), P(None, dp, tensor)),
        check_vma=False,
    )
```

```python
import jax
import jax.numpy as jnp
from jax import lax
from jax.sharding import Mesh, PartitionSpec as P

PATTERN_PAIRS = ((0, 1), (0, 2), (0, 3), (1, 2), (1, 3), (2, 3))
inverse_temp = 0.5
F32, BF16 = jnp.float32, jnp.bfloat16
ORDER = (0, 1, 3, 2)


def soft_mask(logits, gumbel):
    exponent = jnp.exp((logits + gumbel) * inverse_temp)
    chances = exponent / jnp.sum(exponent, axis=0)
    kept_slots = []
    for position in range(4):
        chosen = [chances[which] for which in range(6) if position in PATTERN_PAIRS[which]]
        kept_slots.append(chosen[0] + chosen[1] + chosen[2])
    mask_full = jnp.stack(kept_slots, axis=1)
    return (chances, mask_full.reshape(-1, mask_full.shape[2]))


def logit_grads(chances, mask_grad):
    groups = mask_grad.reshape(-1, 4, mask_grad.shape[1])
    pattern = jnp.stack(
        [
            groups[:, first_slot] + groups[:, second_slot]
            for first_slot, second_slot in PATTERN_PAIRS
        ],
        axis=0,
    )
    average = jnp.sum(chances * pattern, axis=0)
    return chances * (pattern - average) * inverse_temp


def shift(value, axis, by):
    size = lax.axis_size(axis)
    return lax.ppermute(value, axis, [(i, (i + by) % size) for i in range(size)])


def tie(*values):
    return lax.optimization_barrier(values)


def input_part(mine, its, masked, x):
    given = lax.dot_general(
        its, masked, (((1,), (1,)), ((), ())), preferred_element_type=F32
    ).astype(BF16)
    given = shift(given, "c", 1)
    kept = lax.dot_general(mine, masked, (((1,), (1,)), ((), ())), preferred_element_type=F32)
    total = (kept + given.astype(F32)).reshape(4, 4, mine.shape[0] // 16, masked.shape[0])
    base = lax.dynamic_index_in_dim(total, x, 1, False)
    total = total.astype(BF16)
    sent = [lax.dynamic_index_in_dim(total, (x - j) % 4, 1, False) for j in (1, 2, 3)]
    return base, *sent


def body(activations, token_scales, out_grad, weight, logits, gumbel):
    y, zl, x = lax.axis_index("y"), lax.axis_index("zl"), lax.axis_index("x")
    zh, core = lax.axis_index("zh"), lax.axis_index("c")
    rows, features = activations.shape
    depth, hidden = weight.shape
    wide = 4 * depth

    own = out_grad.reshape(8, 2, rows, hidden).transpose(1, 0, 2, 3).reshape(16 * rows, hidden)
    half = 8 * rows

    local = (activations.astype(F32) * token_scales[:, None]).astype(BF16)
    pieces = []
    for k in ORDER:
        pieces.append(
            jnp.concatenate(
                [
                    lax.dynamic_slice_in_dim(
                        local, ((y + k) % 4) * wide + ((zl + m) % 4) * depth, depth, 1
                    )
                    for m in range(4)
                ],
                axis=1,
            )
        )
    local = jnp.stack(pieces, axis=0)

    other = shift(local, "zh", 1)
    below, above = shift(own, "y", 1), shift(own, "y", -1)
    chances, mask_full = soft_mask(logits, gumbel)
    weight_wide = weight.astype(F32)
    masked = (weight_wide * mask_full).astype(BF16)
    other, below, above, own = tie(other, below, above, own)

    masked_1 = shift(masked, "zl", -1)
    far = shift(own, "y", 2)
    scaled = []
    for place, k in enumerate(ORDER):
        mine, its = local[place], other[place]
        piece = jnp.stack([jnp.where(zh == 0, mine, its), jnp.where(zh == 0, its, mine)], axis=0)
        scaled.append(shift(piece, "y", k) if k else piece)
    masked_1, *scaled = tie(masked_1, *scaled)
    scaled = jnp.stack(scaled, axis=0).reshape(4, 2 * rows, wide)

    masked_2 = shift(masked_1, "zl", -1)
    scaled_1, scaled_3 = shift(scaled, "x", 1), shift(scaled, "x", 3)
    pair = jnp.concatenate([masked, masked_1], axis=0)
    pair, masked_2, far, scaled, scaled_1, scaled_3 = tie(
        pair, masked_2, far, scaled, scaled_1, scaled_3
    )

    masked_3 = shift(masked_2, "zl", -1)
    scaled_2 = shift(scaled, "x", 2)
    near = (scaled, scaled_1, scaled_3)
    near_core = shift(jnp.stack(near, axis=0), "c", 1)
    near_core, far = tie(near_core, far)
    grads = jnp.concatenate([own, below, above, far], axis=0)
    halves = grads.reshape(4, 2, half, hidden)
    mine = lax.dynamic_index_in_dim(halves, core, 1, False).reshape(4 * half, hidden)
    its = lax.dynamic_index_in_dim(halves, 1 - core, 1, False).reshape(4 * half, hidden)
    base_1, *first = input_part(mine, its, pair, x)
    masked_3, scaled_2, base_1, *first = tie(masked_3, scaled_2, base_1, *first)

    far_core = shift(scaled_2, "c", 1)
    first = [shift(first[j - 1], "x", -j) for j in (1, 2, 3)]
    pair = jnp.concatenate([masked_2, masked_3], axis=0)
    base_2, *second = input_part(mine, its, pair, x)
    out = tie(*first, *second)
    first, second = out[:3], out[3:]
    rows_of = jnp.zeros((4, 2, 4, 2 * rows, wide), BF16)
    for part, j, on_core in (
        (near[0], 0, core),
        (near[1], 1, core),
        (near[2], 3, core),
        (near_core[0], 0, 1 - core),
        (near_core[1], 1, 1 - core),
        (near_core[2], 3, 1 - core),
        (scaled_2, 2, core),
        (far_core, 2, 1 - core),
    ):
        part = part[:, None, None]
        rows_of = lax.dynamic_update_slice(rows_of, part, (0, on_core, (x - j) % 4, 0, 0))
    scaled = rows_of.reshape(4 * 16 * rows, wide)

    grad_w = [
        lax.dot_general(
            scaled[:, m * depth : (m + 1) * depth],
            grads,
            (((0,), (0,)), ((), ())),
            preferred_element_type=F32,
        )
        for m in range(4)
    ]
    moving = grad_w[1].astype(BF16)

    for m in (2, 3):
        moving = (shift(moving, "zl", -1).astype(F32) + grad_w[m]).astype(BF16)
    moving = shift(moving, "zl", -1)

    second = [shift(second[j - 1], "x", -j) for j in (1, 2, 3)]

    total = jnp.concatenate(
        [
            base + parts[0].astype(F32) + parts[1].astype(F32) + parts[2].astype(F32)
            for base, parts in ((base_1, first), (base_2, second))
        ],
        axis=-1,
    ).reshape(4, 2, rows, wide)
    other = shift(lax.dynamic_index_in_dim(total, 1 - zh, 1, False).astype(BF16), "zh", 1)

    total = lax.dynamic_index_in_dim(total, zh, 1, False) + other.astype(F32)
    total = total.astype(BF16)
    total = jnp.concatenate([total, total], axis=2)
    total = lax.dynamic_slice_in_dim(total, ((4 - zl) % 4) * depth, wide, 2)
    input_grad = jnp.zeros((rows, features), BF16)
    for place, k in enumerate(ORDER):
        part = shift(total[place], "y", -k) if k else total[place]
        input_grad = lax.dynamic_update_slice(input_grad, part, (0, ((y + k) % 4) * wide))

    return (input_grad, logit_grads(chances, (moving.astype(F32) + grad_w[0]) * weight_wide))


def solution(mesh):
    fine = Mesh(mesh.devices.reshape(4, 4, 4, 2, 2), ("y", "zl", "x", "zh", "c"))
    dp, tensor = ("y", "zl"), ("x", "zh", "c")
    return jax.shard_map(
        body,
        mesh=fine,
        in_specs=(
            P(dp + tensor, None),
            P(dp + tensor),
            P(dp, tensor),
            P(dp, tensor),
            P(None, dp, tensor),
            P(None, dp, tensor),
        ),
        out_specs=(P(dp + tensor, None), P(None, dp, tensor)),
        check_vma=False,
    )
```

```python
import jax
import jax.numpy as jnp
from jax import lax
from jax.sharding import Mesh, PartitionSpec as P

PATTERN_PAIRS = ((0, 1), (0, 2), (0, 3), (1, 2), (1, 3), (2, 3))
inverse_temp = 0.5
F32, BF16 = jnp.float32, jnp.bfloat16


def soft_mask(logits, gumbel):
    exponent = jnp.exp((logits + gumbel) * inverse_temp)
    chances = exponent / jnp.sum(exponent, axis=0)
    kept_slots = []
    for position in range(4):
        chosen = [chances[which] for which in range(6) if position in PATTERN_PAIRS[which]]
        kept_slots.append(chosen[0] + chosen[1] + chosen[2])
    mask_full = jnp.stack(kept_slots, axis=1)
    return (chances, mask_full.reshape(-1, mask_full.shape[2]))


def logit_grads(chances, mask_grad):
    groups = mask_grad.reshape(-1, 4, mask_grad.shape[1])
    pattern = jnp.stack(
        [
            groups[:, first_slot] + groups[:, second_slot]
            for first_slot, second_slot in PATTERN_PAIRS
        ],
        axis=0,
    )
    average = jnp.sum(chances * pattern, axis=0)
    return chances * (pattern - average) * inverse_temp


def shift(value, axis, by):
    size = lax.axis_size(axis)
    return lax.ppermute(value, axis, [(i, (i + by) % size) for i in range(size)])


def tie(*values):
    return lax.optimization_barrier(values)


def in_place(parts, which):
    which = which.reshape((-1,) + (1,) * parts[0].ndim)
    placed = parts[0][None]
    for k in range(1, len(parts)):
        placed = jnp.where(which == k, parts[k][None], placed)
    return placed


def body(activations, token_scales, out_grad, weight, logits, gumbel):
    y, zl, x = lax.axis_index("y"), lax.axis_index("zl"), lax.axis_index("x")
    zh, core = lax.axis_index("zh"), lax.axis_index("c")
    rows, features = activations.shape
    depth, hidden = weight.shape
    wide = 4 * depth

    own = out_grad.reshape(8, 2, rows, hidden).transpose(1, 0, 2, 3).reshape(16 * rows, hidden)
    half = 8 * rows

    local = (activations.astype(F32) * token_scales[:, None]).astype(BF16)
    pieces = []
    for k in range(4):
        pieces.append(
            jnp.concatenate(
                [
                    lax.dynamic_slice_in_dim(
                        local, ((y + k) % 4) * wide + ((zl + m) % 4) * depth, depth, 1
                    )
                    for m in range(4)
                ],
                axis=1,
            )
        )
    scaled = jnp.stack([pieces[0]] + [shift(pieces[k], "y", k) for k in (1, 2, 3)], axis=0)
    scaled, own = tie(scaled, own)

    chances, mask_full = soft_mask(logits, gumbel)
    weight_wide = weight.astype(F32)
    masked = (weight_wide * mask_full).astype(BF16)

    other = shift(scaled, "zh", 1)
    masked_1 = shift(masked, "zl", -1)
    below, above = shift(own, "y", 1), shift(own, "y", -1)
    other, masked_1, below, above = tie(other, masked_1, below, above)
    scaled = in_place([scaled, other], jnp.where(zh == 0, jnp.arange(2), 1 - jnp.arange(2)))

    masked_2 = shift(masked_1, "zl", -1)
    far_a, far_b = shift(below[:half], "y", 1), shift(above[half:], "y", -1)
    scaled_1, scaled_3 = shift(scaled, "x", 1), shift(scaled, "x", 3)
    masked_2, far_a, far_b, scaled, scaled_1, scaled_3 = tie(
        masked_2, far_a, far_b, scaled, scaled_1, scaled_3
    )
    grads = jnp.concatenate([own, below, far_a, far_b, above], axis=0)

    masked_3 = shift(masked_2, "zl", -1)
    scaled_2 = shift(scaled, "x", 2)
    near = (scaled, scaled_1, scaled_3)
    near_core = shift(jnp.stack(near, axis=0), "c", 1)
    scaled_2, near_core = tie(scaled_2, near_core)
    far_core = shift(scaled_2, "c", 1)
    rows_of = jnp.zeros((4, 2, 4, 2, rows, wide), BF16)
    for part, j, on_core in (
        (near[0], 0, core),
        (near[1], 1, core),
        (near[2], 3, core),
        (near_core[0], 0, 1 - core),
        (near_core[1], 1, 1 - core),
        (near_core[2], 3, 1 - core),
        (scaled_2, 2, core),
        (far_core, 2, 1 - core),
    ):
        part = part.transpose(1, 0, 2, 3)[:, None, None]
        rows_of = lax.dynamic_update_slice(rows_of, part, (0, on_core, (x - j) % 4, 0, 0, 0))
    scaled = rows_of.reshape(4 * 16 * rows, wide)

    grad_w = [
        lax.dot_general(
            scaled[:, m * depth : (m + 1) * depth],
            grads,
            (((0,), (0,)), ((), ())),
            preferred_element_type=F32,
        )
        for m in range(4)
    ]
    moving = grad_w[1].astype(BF16)

    grads = grads.reshape(4, 2, half, hidden)
    mine = lax.dynamic_index_in_dim(grads, core, 1, False).reshape(4 * half, hidden)
    its = lax.dynamic_index_in_dim(grads, 1 - core, 1, False).reshape(4 * half, hidden)
    sent, totals = [], []
    for pair in ((masked, masked_1), (masked_2, masked_3)):
        pair = jnp.concatenate(pair, axis=0)
        given = lax.dot_general(
            its, pair, (((1,), (1,)), ((), ())), preferred_element_type=F32
        ).astype(BF16)
        given = shift(given, "c", 1)
        kept = lax.dot_general(
            mine, pair, (((1,), (1,)), ((), ())), preferred_element_type=F32
        )
        total = (kept + given.astype(F32)).reshape(4, 4, 2 * rows, 2 * depth)
        totals.append(lax.dynamic_index_in_dim(total, x, 1, False))
        total = total.astype(BF16)
        sent.append([lax.dynamic_index_in_dim(total, (x - j) % 4, 1, False) for j in (1, 2, 3)])

    for m in (2, 3):
        moving = (shift(moving, "zl", -1).astype(F32) + grad_w[m]).astype(BF16)
    moving = shift(moving, "zl", -1)

    first = [shift(sent[0][j - 1], "x", -j) for j in (1, 2, 3)]
    out = tie(*first, *sent[1])
    first, second = out[:3], out[3:]
    second = [shift(second[j - 1], "x", -j) for j in (1, 2, 3)]

    total = jnp.concatenate(
        [
            base + parts[0].astype(F32) + parts[1].astype(F32) + parts[2].astype(F32)
            for base, parts in zip(totals, (first, second))
        ],
        axis=-1,
    ).reshape(4, 2, rows, wide)
    other = shift(lax.dynamic_index_in_dim(total, 1 - zh, 1, False).astype(BF16), "zh", 1)

    total = lax.dynamic_index_in_dim(total, zh, 1, False) + other.astype(F32)
    total = total.astype(BF16)
    total = jnp.concatenate([total, total], axis=2)
    total = lax.dynamic_slice_in_dim(total, ((4 - zl) % 4) * depth, wide, 2)
    parts = [total[0]] + [shift(total[k], "y", -k) for k in (1, 2, 3)]
    input_grad = jnp.zeros((rows, features), BF16)
    for k in range(4):
        input_grad = lax.dynamic_update_slice(input_grad, parts[k], (0, ((y + k) % 4) * wide))

    return (input_grad, logit_grads(chances, (moving.astype(F32) + grad_w[0]) * weight_wide))


def solution(mesh):
    fine = Mesh(mesh.devices.reshape(4, 4, 4, 2, 2), ("y", "zl", "x", "zh", "c"))
    dp, tensor = ("y", "zl"), ("x", "zh", "c")
    return jax.shard_map(
        body,
        mesh=fine,
        in_specs=(
            P(dp + tensor, None),
            P(dp + tensor),
            P(dp, tensor),
            P(dp, tensor),
            P(None, dp, tensor),
            P(None, dp, tensor),
        ),
        out_specs=(P(dp + tensor, None), P(None, dp, tensor)),
        check_vma=False,
    )
```

```python
import jax
import jax.numpy as jnp
from jax import lax
from jax.sharding import Mesh, PartitionSpec as P

PATTERN_PAIRS = ((0, 1), (0, 2), (0, 3), (1, 2), (1, 3), (2, 3))
inverse_temp = 0.5
F32, BF16 = jnp.float32, jnp.bfloat16


def soft_mask(logits, gumbel):
    exponent = jnp.exp((logits + gumbel) * inverse_temp)
    chances = exponent / jnp.sum(exponent, axis=0)
    kept_slots = []
    for position in range(4):
        chosen = [chances[which] for which in range(6) if position in PATTERN_PAIRS[which]]
        kept_slots.append(chosen[0] + chosen[1] + chosen[2])
    mask_full = jnp.stack(kept_slots, axis=1)
    return (chances, mask_full.reshape(-1, mask_full.shape[2]))


def logit_grads(chances, mask_grad):
    groups = mask_grad.reshape(-1, 4, mask_grad.shape[1])
    pattern = jnp.stack(
        [
            groups[:, first_slot] + groups[:, second_slot]
            for first_slot, second_slot in PATTERN_PAIRS
        ],
        axis=0,
    )
    average = jnp.sum(chances * pattern, axis=0)
    return chances * (pattern - average) * inverse_temp


def shift(value, axis, by):
    size = lax.axis_size(axis)
    return lax.ppermute(value, axis, [(i, (i + by) % size) for i in range(size)])


def tie(*values):
    return lax.optimization_barrier(values)


def in_place(parts, which):
    which = which.reshape((-1,) + (1,) * parts[0].ndim)
    placed = parts[0][None]
    for k in range(1, len(parts)):
        placed = jnp.where(which == k, parts[k][None], placed)
    return placed


def body(activations, token_scales, out_grad, weight, logits, gumbel):
    y, zl, x = lax.axis_index("y"), lax.axis_index("zl"), lax.axis_index("x")
    zh, core = lax.axis_index("zh"), lax.axis_index("c")
    rows, features = activations.shape
    depth, hidden = weight.shape
    wide = 4 * depth

    own = out_grad.reshape(8, 2, rows, hidden).transpose(1, 0, 2, 3).reshape(16 * rows, hidden)
    half = 8 * rows

    local = (activations.astype(F32) * token_scales[:, None]).astype(BF16)
    pieces = []
    for k in range(4):
        pieces.append(
            jnp.concatenate(
                [
                    lax.dynamic_slice_in_dim(
                        local, ((y + k) % 4) * wide + ((zl + m) % 4) * depth, depth, 1
                    )
                    for m in range(4)
                ],
                axis=1,
            )
        )
    scaled = jnp.stack([pieces[0]] + [shift(pieces[k], "y", k) for k in (1, 2, 3)], axis=0)
    scaled, own = tie(scaled, own)

    chances, mask_full = soft_mask(logits, gumbel)
    weight_wide = weight.astype(F32)
    masked = (weight_wide * mask_full).astype(BF16)

    other = shift(scaled, "zh", 1)
    masked_1 = shift(masked, "zl", -1)
    below, above = shift(own, "y", 1), shift(own, "y", -1)
    other, masked_1, below, above = tie(other, masked_1, below, above)
    scaled = in_place([scaled, other], jnp.where(zh == 0, jnp.arange(2), 1 - jnp.arange(2)))

    masked_2 = shift(masked_1, "zl", -1)
    far_a, far_b = shift(below[:half], "y", 1), shift(above[half:], "y", -1)
    scaled_1, scaled_3 = shift(scaled, "x", 1), shift(scaled, "x", 3)
    masked_2, far_a, far_b, scaled, scaled_1, scaled_3 = tie(
        masked_2, far_a, far_b, scaled, scaled_1, scaled_3
    )
    grads = jnp.concatenate([own, below, far_a, far_b, above], axis=0)

    masked_3 = shift(masked_2, "zl", -1)
    scaled_2 = shift(scaled, "x", 2)
    near = (scaled, scaled_1, scaled_3)
    near_core = shift(jnp.stack(near, axis=0), "c", 1)
    scaled_2, near_core = tie(scaled_2, near_core)
    far_core = shift(scaled_2, "c", 1)
    rows_of = jnp.zeros((4, 2, 4, 2, rows, wide), BF16)
    for part, j, on_core in (
        (near[0], 0, core),
        (near[1], 1, core),
        (near[2], 3, core),
        (near_core[0], 0, 1 - core),
        (near_core[1], 1, 1 - core),
        (near_core[2], 3, 1 - core),
        (scaled_2, 2, core),
        (far_core, 2, 1 - core),
    ):
        part = part.transpose(1, 0, 2, 3)[:, None, None]
        rows_of = lax.dynamic_update_slice(rows_of, part, (0, on_core, (x - j) % 4, 0, 0, 0))
    scaled = rows_of.reshape(4 * 16 * rows, wide)

    grad_w = [
        lax.dot_general(
            scaled[:, m * depth : (m + 1) * depth],
            grads,
            (((0,), (0,)), ((), ())),
            preferred_element_type=F32,
        )
        for m in range(4)
    ]
    moving = grad_w[1].astype(BF16)

    grads = grads.reshape(4, 2, half, hidden)
    mine = lax.dynamic_index_in_dim(grads, core, 1, False).reshape(4 * half, hidden)
    its = lax.dynamic_index_in_dim(grads, 1 - core, 1, False).reshape(4 * half, hidden)
    sent, totals = [], []
    for pair in ((masked, masked_1), (masked_2, masked_3)):
        pair = jnp.concatenate(pair, axis=0)
        given = lax.dot_general(
            its, pair, (((1,), (1,)), ((), ())), preferred_element_type=F32
        ).astype(BF16)
        given = shift(given, "c", 1)
        kept = lax.dot_general(
            mine, pair, (((1,), (1,)), ((), ())), preferred_element_type=F32
        )
        total = (kept + given.astype(F32)).reshape(4, 4, 2 * rows, 2 * depth)
        totals.append(lax.dynamic_index_in_dim(total, x, 1, False))
        total = total.astype(BF16)
        sent.append([lax.dynamic_index_in_dim(total, (x - j) % 4, 1, False) for j in (1, 2, 3)])

    moving = (shift(moving, "zl", -1).astype(F32) + grad_w[2]).astype(BF16)

    first = [shift(sent[0][j - 1], "x", -j) for j in (1, 2, 3)]
    out = tie(*first, *sent[1])
    first, second = out[:3], out[3:]
    second = [shift(second[j - 1], "x", -j) for j in (1, 2, 3)]
    moving = shift(moving, "zl", -1)
    moving, *second = tie(moving, *second)
    moving = (moving.astype(F32) + grad_w[3]).astype(BF16)

    moving = shift(moving, "zl", -1)

    total = jnp.concatenate(
        [
            base + parts[0].astype(F32) + parts[1].astype(F32) + parts[2].astype(F32)
            for base, parts in zip(totals, (first, second))
        ],
        axis=-1,
    ).reshape(4, 2, rows, wide)
    other = shift(lax.dynamic_index_in_dim(total, 1 - zh, 1, False).astype(BF16), "zh", 1)

    total = lax.dynamic_index_in_dim(total, zh, 1, False) + other.astype(F32)
    total = total.astype(BF16)
    total = jnp.concatenate([total, total], axis=2)
    total = lax.dynamic_slice_in_dim(total, ((4 - zl) % 4) * depth, wide, 2)
    parts = [total[0]] + [shift(total[k], "y", -k) for k in (1, 2, 3)]
    input_grad = jnp.zeros((rows, features), BF16)
    for k in range(4):
        input_grad = lax.dynamic_update_slice(input_grad, parts[k], (0, ((y + k) % 4) * wide))

    return (input_grad, logit_grads(chances, (moving.astype(F32) + grad_w[0]) * weight_wide))


def solution(mesh):
    fine = Mesh(mesh.devices.reshape(4, 4, 4, 2, 2), ("y", "zl", "x", "zh", "c"))
    dp, tensor = ("y", "zl"), ("x", "zh", "c")
    return jax.shard_map(
        body,
        mesh=fine,
        in_specs=(
            P(dp + tensor, None),
            P(dp + tensor),
            P(dp, tensor),
            P(dp, tensor),
            P(None, dp, tensor),
            P(None, dp, tensor),
        ),
        out_specs=(P(dp + tensor, None), P(None, dp, tensor)),
        check_vma=False,
    )
```

```python
import jax
import jax.numpy as jnp
from jax import lax
from jax.sharding import Mesh, PartitionSpec as P

PATTERN_PAIRS = ((0, 1), (0, 2), (0, 3), (1, 2), (1, 3), (2, 3))
inverse_temp = 0.5
F32, BF16 = jnp.float32, jnp.bfloat16
ORDER = (0, 1, 3, 2)


def soft_mask(logits, gumbel):
    exponent = jnp.exp((logits + gumbel) * inverse_temp)
    chances = exponent / jnp.sum(exponent, axis=0)
    kept_slots = []
    for position in range(4):
        chosen = [chances[which] for which in range(6) if position in PATTERN_PAIRS[which]]
        kept_slots.append(chosen[0] + chosen[1] + chosen[2])
    mask_full = jnp.stack(kept_slots, axis=1)
    return (chances, mask_full.reshape(-1, mask_full.shape[2]))


def logit_grads(chances, mask_grad):
    groups = mask_grad.reshape(-1, 4, mask_grad.shape[1])
    pattern = jnp.stack(
        [
            groups[:, first_slot] + groups[:, second_slot]
            for first_slot, second_slot in PATTERN_PAIRS
        ],
        axis=0,
    )
    average = jnp.sum(chances * pattern, axis=0)
    return chances * (pattern - average) * inverse_temp


def shift(value, axis, by):
    size = lax.axis_size(axis)
    return lax.ppermute(value, axis, [(i, (i + by) % size) for i in range(size)])


def tie(*values):
    return lax.optimization_barrier(values)


def in_place(parts, which):
    which = which.reshape((-1,) + (1,) * parts[0].ndim)
    placed = parts[0][None]
    for k in range(1, len(parts)):
        placed = jnp.where(which == k, parts[k][None], placed)
    return placed


def body(activations, token_scales, out_grad, weight, logits, gumbel):
    y, zl, x = lax.axis_index("y"), lax.axis_index("zl"), lax.axis_index("x")
    zh, core = lax.axis_index("zh"), lax.axis_index("c")
    rows, features = activations.shape
    depth, hidden = weight.shape
    wide = 4 * depth

    own = out_grad.reshape(8, 2, rows, hidden).transpose(1, 0, 2, 3).reshape(16 * rows, hidden)
    half = 8 * rows

    local = (activations.astype(F32) * token_scales[:, None]).astype(BF16)
    pieces = []
    for k in ORDER:
        pieces.append(
            jnp.concatenate(
                [
                    lax.dynamic_slice_in_dim(
                        local, ((y + k) % 4) * wide + ((zl + m) % 4) * depth, depth, 1
                    )
                    for m in range(4)
                ],
                axis=1,
            )
        )
    scaled = jnp.stack(
        [pieces[0]] + [shift(part, "y", k) for part, k in zip(pieces[1:], ORDER[1:])], axis=0
    )
    scaled, own = tie(scaled, own)

    chances, mask_full = soft_mask(logits, gumbel)
    weight_wide = weight.astype(F32)
    masked = (weight_wide * mask_full).astype(BF16)

    other = shift(scaled, "zh", 1)
    masked_1 = shift(masked, "zl", -1)
    below, above = shift(own, "y", 1), shift(own, "y", -1)
    below_half, above_half = below[:half], above[half:]
    other, masked_1, below, above, below_half, above_half = tie(
        other, masked_1, below, above, below_half, above_half
    )
    scaled = in_place([scaled, other], jnp.where(zh == 0, jnp.arange(2), 1 - jnp.arange(2)))

    masked_2 = shift(masked_1, "zl", -1)
    far_a, far_b = shift(below_half, "y", 1), shift(above_half, "y", -1)
    scaled_1, scaled_3 = shift(scaled, "x", 1), shift(scaled, "x", 3)
    masked_2, far_a, far_b, scaled, scaled_1, scaled_3 = tie(
        masked_2, far_a, far_b, scaled, scaled_1, scaled_3
    )
    grads = jnp.concatenate([own, below, above, far_a, far_b], axis=0)

    masked_3 = shift(masked_2, "zl", -1)
    scaled_2 = shift(scaled, "x", 2)
    near = (scaled, scaled_1, scaled_3)
    near_core = shift(jnp.stack(near, axis=0), "c", 1)
    scaled_2, near_core = tie(scaled_2, near_core)
    far_core = shift(scaled_2, "c", 1)
    rows_of = jnp.zeros((4, 2, 4, 2, rows, wide), BF16)
    for part, j, on_core in (
        (near[0], 0, core),
        (near[1], 1, core),
        (near[2], 3, core),
        (near_core[0], 0, 1 - core),
        (near_core[1], 1, 1 - core),
        (near_core[2], 3, 1 - core),
        (scaled_2, 2, core),
        (far_core, 2, 1 - core),
    ):
        part = part.transpose(1, 0, 2, 3)[:, None, None]
        rows_of = lax.dynamic_update_slice(rows_of, part, (0, on_core, (x - j) % 4, 0, 0, 0))
    scaled = rows_of.reshape(4 * 16 * rows, wide)

    grad_w = [
        lax.dot_general(
            scaled[:, m * depth : (m + 1) * depth],
            grads,
            (((0,), (0,)), ((), ())),
            preferred_element_type=F32,
        )
        for m in range(4)
    ]
    moving = grad_w[1].astype(BF16)

    grads = grads.reshape(4, 2, half, hidden)
    mine = lax.dynamic_index_in_dim(grads, core, 1, False).reshape(4 * half, hidden)
    its = lax.dynamic_index_in_dim(grads, 1 - core, 1, False).reshape(4 * half, hidden)
    sent, totals = [], []
    for pair in ((masked, masked_1), (masked_2, masked_3)):
        pair = jnp.concatenate(pair, axis=0)
        given = lax.dot_general(
            its, pair, (((1,), (1,)), ((), ())), preferred_element_type=F32
        ).astype(BF16)
        given = shift(given, "c", 1)
        kept = lax.dot_general(
            mine, pair, (((1,), (1,)), ((), ())), preferred_element_type=F32
        )
        total = (kept + given.astype(F32)).reshape(4, 4, 2 * rows, 2 * depth)
        totals.append(lax.dynamic_index_in_dim(total, x, 1, False))
        total = total.astype(BF16)
        sent.append([lax.dynamic_index_in_dim(total, (x - j) % 4, 1, False) for j in (1, 2, 3)])

    moving = (shift(moving, "zl", -1).astype(F32) + grad_w[2]).astype(BF16)

    first = [shift(sent[0][j - 1], "x", -j) for j in (1, 2, 3)]
    out = tie(*first, *sent[1])
    first, second = out[:3], out[3:]
    second = [shift(second[j - 1], "x", -j) for j in (1, 2, 3)]
    moving = shift(moving, "zl", -1)
    moving, *second = tie(moving, *second)
    moving = (moving.astype(F32) + grad_w[3]).astype(BF16)

    total = jnp.concatenate(
        [
            base + parts[0].astype(F32) + parts[1].astype(F32) + parts[2].astype(F32)
            for base, parts in zip(totals, (first, second))
        ],
        axis=-1,
    ).reshape(4, 2, rows, wide)
    other = shift(lax.dynamic_index_in_dim(total, 1 - zh, 1, False).astype(BF16), "zh", 1)
    moving = shift(moving, "zl", -1)
    other, moving = tie(other, moving)

    total = lax.dynamic_index_in_dim(total, zh, 1, False) + other.astype(F32)
    total = total.astype(BF16)
    total = jnp.concatenate([total, total], axis=2)
    total = lax.dynamic_slice_in_dim(total, ((4 - zl) % 4) * depth, wide, 2)
    input_grad = jnp.zeros((rows, features), BF16)
    for place, k in enumerate(ORDER):
        part = shift(total[place], "y", -k) if k else total[place]
        input_grad = lax.dynamic_update_slice(input_grad, part, (0, ((y + k) % 4) * wide))

    return (input_grad, logit_grads(chances, (moving.astype(F32) + grad_w[0]) * weight_wide))


def solution(mesh):
    fine = Mesh(mesh.devices.reshape(4, 4, 4, 2, 2), ("y", "zl", "x", "zh", "c"))
    dp, tensor = ("y", "zl"), ("x", "zh", "c")
    return jax.shard_map(
        body,
        mesh=fine,
        in_specs=(
            P(dp + tensor, None),
            P(dp + tensor),
            P(dp, tensor),
            P(dp, tensor),
            P(None, dp, tensor),
            P(None, dp, tensor),
        ),
        out_specs=(P(dp + tensor, None), P(None, dp, tensor)),
        check_vma=False,
    )
```

```python
import jax
import jax.numpy as jnp
from jax import lax
from jax.sharding import Mesh, PartitionSpec as P

PATTERN_PAIRS = ((0, 1), (0, 2), (0, 3), (1, 2), (1, 3), (2, 3))
inverse_temp = 0.5
F32, BF16 = jnp.float32, jnp.bfloat16


def soft_mask(logits, gumbel):
    exponent = jnp.exp((logits + gumbel) * inverse_temp)
    chances = exponent / jnp.sum(exponent, axis=0)
    kept_slots = []
    for position in range(4):
        chosen = [chances[which] for which in range(6) if position in PATTERN_PAIRS[which]]
        kept_slots.append(chosen[0] + chosen[1] + chosen[2])
    mask_full = jnp.stack(kept_slots, axis=1)
    return (chances, mask_full.reshape(-1, mask_full.shape[2]))


def logit_grads(chances, mask_grad):
    groups = mask_grad.reshape(-1, 4, mask_grad.shape[1])
    pattern = jnp.stack(
        [
            groups[:, first_slot] + groups[:, second_slot]
            for first_slot, second_slot in PATTERN_PAIRS
        ],
        axis=0,
    )
    average = jnp.sum(chances * pattern, axis=0)
    return chances * (pattern - average) * inverse_temp


def shift(value, axis, by):
    size = lax.axis_size(axis)
    return lax.ppermute(value, axis, [(i, (i + by) % size) for i in range(size)])


def tie(*values):
    return lax.optimization_barrier(values)


def in_place(parts, which):
    which = which.reshape((-1,) + (1,) * parts[0].ndim)
    placed = parts[0][None]
    for k in range(1, len(parts)):
        placed = jnp.where(which == k, parts[k][None], placed)
    return placed


def body(activations, token_scales, out_grad, weight, logits, gumbel):
    y, zl, x = lax.axis_index("y"), lax.axis_index("zl"), lax.axis_index("x")
    zh, core = lax.axis_index("zh"), lax.axis_index("c")
    rows, features = activations.shape
    depth, hidden = weight.shape
    wide = 4 * depth

    own = out_grad.reshape(8, 2, rows, hidden).transpose(1, 0, 2, 3).reshape(16 * rows, hidden)
    half = 8 * rows

    local = (activations.astype(F32) * token_scales[:, None]).astype(BF16)
    pieces = []
    for k in range(4):
        pieces.append(
            jnp.concatenate(
                [
                    lax.dynamic_slice_in_dim(
                        local, ((y + k) % 4) * wide + ((zl + m) % 4) * depth, depth, 1
                    )
                    for m in range(4)
                ],
                axis=1,
            )
        )
    scaled = jnp.stack([pieces[0]] + [shift(pieces[k], "y", k) for k in (1, 2, 3)], axis=0)
    scaled, own = tie(scaled, own)

    chances, mask_full = soft_mask(logits, gumbel)
    weight_wide = weight.astype(F32)
    masked = (weight_wide * mask_full).astype(BF16)

    other = shift(scaled, "zh", 1)
    masked_1 = shift(masked, "zl", -1)
    below, above = shift(own, "y", 1), shift(own, "y", -1)
    below_half, above_half = below[:half], above[half:]
    other, masked_1, below, above, below_half, above_half = tie(
        other, masked_1, below, above, below_half, above_half
    )
    scaled = in_place([scaled, other], jnp.where(zh == 0, jnp.arange(2), 1 - jnp.arange(2)))

    masked_2 = shift(masked_1, "zl", -1)
    far_a, far_b = shift(below_half, "y", 1), shift(above_half, "y", -1)
    scaled_1, scaled_3 = shift(scaled, "x", 1), shift(scaled, "x", 3)
    masked_2, far_a, far_b, scaled, scaled_1, scaled_3 = tie(
        masked_2, far_a, far_b, scaled, scaled_1, scaled_3
    )
    grads = jnp.concatenate([own, below, far_a, far_b, above], axis=0)

    masked_3 = shift(masked_2, "zl", -1)
    scaled_2 = shift(scaled, "x", 2)
    near = (scaled, scaled_1, scaled_3)
    near_core = shift(jnp.stack(near, axis=0), "c", 1)
    scaled_2, near_core = tie(scaled_2, near_core)
    far_core = shift(scaled_2, "c", 1)
    rows_of = jnp.zeros((4, 2, 4, 2, rows, wide), BF16)
    for part, j, on_core in (
        (near[0], 0, core),
        (near[1], 1, core),
        (near[2], 3, core),
        (near_core[0], 0, 1 - core),
        (near_core[1], 1, 1 - core),
        (near_core[2], 3, 1 - core),
        (scaled_2, 2, core),
        (far_core, 2, 1 - core),
    ):
        part = part.transpose(1, 0, 2, 3)[:, None, None]
        rows_of = lax.dynamic_update_slice(rows_of, part, (0, on_core, (x - j) % 4, 0, 0, 0))
    scaled = rows_of.reshape(4 * 16 * rows, wide)

    grad_w = [
        lax.dot_general(
            scaled[:, m * depth : (m + 1) * depth],
            grads,
            (((0,), (0,)), ((), ())),
            preferred_element_type=F32,
        )
        for m in range(4)
    ]
    moving = grad_w[1].astype(BF16)

    grads = grads.reshape(4, 2, half, hidden)
    mine = lax.dynamic_index_in_dim(grads, core, 1, False).reshape(4 * half, hidden)
    its = lax.dynamic_index_in_dim(grads, 1 - core, 1, False).reshape(4 * half, hidden)
    sent, totals = [], []
    for pair in ((masked, masked_1), (masked_2, masked_3)):
        pair = jnp.concatenate(pair, axis=0)
        given = lax.dot_general(
            its, pair, (((1,), (1,)), ((), ())), preferred_element_type=F32
        ).astype(BF16)
        given = shift(given, "c", 1)
        kept = lax.dot_general(
            mine, pair, (((1,), (1,)), ((), ())), preferred_element_type=F32
        )
        total = (kept + given.astype(F32)).reshape(4, 4, 2 * rows, 2 * depth)
        totals.append(lax.dynamic_index_in_dim(total, x, 1, False))
        total = total.astype(BF16)
        sent.append([lax.dynamic_index_in_dim(total, (x - j) % 4, 1, False) for j in (1, 2, 3)])

    moving = (shift(moving, "zl", -1).astype(F32) + grad_w[2]).astype(BF16)

    first = [shift(sent[0][j - 1], "x", -j) for j in (1, 2, 3)]
    out = tie(*first, *sent[1])
    first, second = out[:3], out[3:]
    second = [shift(second[j - 1], "x", -j) for j in (1, 2, 3)]
    moving = shift(moving, "zl", -1)
    moving, *second = tie(moving, *second)
    moving = (moving.astype(F32) + grad_w[3]).astype(BF16)

    moving = shift(moving, "zl", -1)

    total = jnp.concatenate(
        [
            base + parts[0].astype(F32) + parts[1].astype(F32) + parts[2].astype(F32)
            for base, parts in zip(totals, (first, second))
        ],
        axis=-1,
    ).reshape(4, 2, rows, wide)
    other = shift(lax.dynamic_index_in_dim(total, 1 - zh, 1, False).astype(BF16), "zh", 1)

    total = lax.dynamic_index_in_dim(total, zh, 1, False) + other.astype(F32)
    total = total.astype(BF16)
    total = jnp.concatenate([total, total], axis=2)
    total = lax.dynamic_slice_in_dim(total, ((4 - zl) % 4) * depth, wide, 2)
    parts = [total[0]] + [shift(total[k], "y", -k) for k in (1, 2, 3)]
    input_grad = jnp.zeros((rows, features), BF16)
    for k in range(4):
        input_grad = lax.dynamic_update_slice(input_grad, parts[k], (0, ((y + k) % 4) * wide))

    return (input_grad, logit_grads(chances, (moving.astype(F32) + grad_w[0]) * weight_wide))


def solution(mesh):
    fine = Mesh(mesh.devices.reshape(4, 4, 4, 2, 2), ("y", "zl", "x", "zh", "c"))
    dp, tensor = ("y", "zl"), ("x", "zh", "c")
    return jax.shard_map(
        body,
        mesh=fine,
        in_specs=(
            P(dp + tensor, None),
            P(dp + tensor),
            P(dp, tensor),
            P(dp, tensor),
            P(None, dp, tensor),
            P(None, dp, tensor),
        ),
        out_specs=(P(dp + tensor, None), P(None, dp, tensor)),
        check_vma=False,
    )
```

```python
import jax
import jax.numpy as jnp
from jax import lax
from jax.sharding import Mesh, PartitionSpec as P

PATTERN_PAIRS = ((0, 1), (0, 2), (0, 3), (1, 2), (1, 3), (2, 3))
inverse_temp = 0.5
F32, BF16 = jnp.float32, jnp.bfloat16


def soft_mask(logits, gumbel):
    exponent = jnp.exp((logits + gumbel) * inverse_temp)
    chances = exponent / jnp.sum(exponent, axis=0)
    kept_slots = []
    for position in range(4):
        chosen = [chances[which] for which in range(6) if position in PATTERN_PAIRS[which]]
        kept_slots.append(chosen[0] + chosen[1] + chosen[2])
    mask_full = jnp.stack(kept_slots, axis=1)
    return (chances, mask_full.reshape(-1, mask_full.shape[2]))


def logit_grads(chances, mask_grad):
    groups = mask_grad.reshape(-1, 4, mask_grad.shape[1])
    pattern = jnp.stack(
        [
            groups[:, first_slot] + groups[:, second_slot]
            for first_slot, second_slot in PATTERN_PAIRS
        ],
        axis=0,
    )
    average = jnp.sum(chances * pattern, axis=0)
    return chances * (pattern - average) * inverse_temp


def shift(value, axis, by):
    size = lax.axis_size(axis)
    return lax.ppermute(value, axis, [(i, (i + by) % size) for i in range(size)])


def tie(*values):
    return lax.optimization_barrier(values)


def in_place(parts, which):
    which = which.reshape((-1,) + (1,) * parts[0].ndim)
    placed = parts[0][None]
    for k in range(1, len(parts)):
        placed = jnp.where(which == k, parts[k][None], placed)
    return placed


def body(activations, token_scales, out_grad, weight, logits, gumbel):
    y, zl, x = lax.axis_index("y"), lax.axis_index("zl"), lax.axis_index("x")
    zh, core = lax.axis_index("zh"), lax.axis_index("c")
    rows, features = activations.shape
    depth, hidden = weight.shape
    wide = 4 * depth

    own = out_grad.reshape(8, 2, rows, hidden).transpose(1, 0, 2, 3).reshape(16 * rows, hidden)
    half = 8 * rows

    local = (activations.astype(F32) * token_scales[:, None]).astype(BF16)
    pieces = []
    for k in range(4):
        pieces.append(
            jnp.concatenate(
                [
                    lax.dynamic_slice_in_dim(
                        local, ((y + k) % 4) * wide + ((zl + m) % 4) * depth, depth, 1
                    )
                    for m in range(4)
                ],
                axis=1,
            )
        )
    scaled = jnp.stack([pieces[0]] + [shift(pieces[k], "y", k) for k in (1, 2, 3)], axis=0)
    scaled, own = tie(scaled, own)

    chances, mask_full = soft_mask(logits, gumbel)
    weight_wide = weight.astype(F32)
    masked = (weight_wide * mask_full).astype(BF16)

    other = shift(scaled, "zh", 1)
    masked_1 = shift(masked, "zl", -1)
    below, above = shift(own, "y", 1), shift(own, "y", -1)
    below_half, above_half = below[:half], above[half:]
    other, masked_1, below, above, below_half, above_half = tie(
        other, masked_1, below, above, below_half, above_half
    )
    scaled = in_place([scaled, other], jnp.where(zh == 0, jnp.arange(2), 1 - jnp.arange(2)))

    masked_2 = shift(masked_1, "zl", -1)
    far_a, far_b = shift(below_half, "y", 1), shift(above_half, "y", -1)
    scaled_1, scaled_3 = shift(scaled, "x", 1), shift(scaled, "x", 3)
    masked_2, far_a, far_b, scaled, scaled_1, scaled_3 = tie(
        masked_2, far_a, far_b, scaled, scaled_1, scaled_3
    )
    grads = jnp.concatenate([own, below, far_a, far_b, above], axis=0)

    masked_3 = shift(masked_2, "zl", -1)
    scaled_2 = shift(scaled, "x", 2)
    near = (scaled, scaled_1, scaled_3)
    near_core = shift(jnp.stack(near, axis=0), "c", 1)
    scaled_2, near_core = tie(scaled_2, near_core)
    far_core = shift(scaled_2, "c", 1)
    rows_of = jnp.zeros((4, 2, 4, 2, rows, wide), BF16)
    for part, j, on_core in (
        (near[0], 0, core),
        (near[1], 1, core),
        (near[2], 3, core),
        (near_core[0], 0, 1 - core),
        (near_core[1], 1, 1 - core),
        (near_core[2], 3, 1 - core),
        (scaled_2, 2, core),
        (far_core, 2, 1 - core),
    ):
        part = part.transpose(1, 0, 2, 3)[:, None, None]
        rows_of = lax.dynamic_update_slice(rows_of, part, (0, on_core, (x - j) % 4, 0, 0, 0))
    scaled = rows_of.reshape(4 * 16 * rows, wide)

    grad_w = [
        lax.dot_general(
            scaled[:, m * depth : (m + 1) * depth],
            grads,
            (((0,), (0,)), ((), ())),
            preferred_element_type=F32,
        )
        for m in range(4)
    ]
    moving = grad_w[1].astype(BF16)
    moving, masked_3 = tie(moving, masked_3)

    grads = grads.reshape(4, 2, half, hidden)
    mine = lax.dynamic_index_in_dim(grads, core, 1, False).reshape(4 * half, hidden)
    its = lax.dynamic_index_in_dim(grads, 1 - core, 1, False).reshape(4 * half, hidden)
    sent, totals = [], []
    for pair in ((masked, masked_1), (masked_2, masked_3)):
        pair = jnp.concatenate(pair, axis=0)
        given = lax.dot_general(
            its, pair, (((1,), (1,)), ((), ())), preferred_element_type=F32
        ).astype(BF16)
        given = shift(given, "c", 1)
        kept = lax.dot_general(
            mine, pair, (((1,), (1,)), ((), ())), preferred_element_type=F32
        )
        total = (kept + given.astype(F32)).reshape(4, 4, 2 * rows, 2 * depth)
        totals.append(lax.dynamic_index_in_dim(total, x, 1, False))
        total = total.astype(BF16)
        sent.append([lax.dynamic_index_in_dim(total, (x - j) % 4, 1, False) for j in (1, 2, 3)])

    moving = (shift(moving, "zl", -1).astype(F32) + grad_w[2]).astype(BF16)

    first = [shift(sent[0][j - 1], "x", -j) for j in (1, 2, 3)]
    out = tie(*first, *sent[1])
    first, second = out[:3], out[3:]
    second = [shift(second[j - 1], "x", -j) for j in (1, 2, 3)]
    moving = shift(moving, "zl", -1)
    moving, *second = tie(moving, *second)
    moving = (moving.astype(F32) + grad_w[3]).astype(BF16)

    moving = shift(moving, "zl", -1)

    total = jnp.concatenate(
        [
            base + parts[0].astype(F32) + parts[1].astype(F32) + parts[2].astype(F32)
            for base, parts in zip(totals, (first, second))
        ],
        axis=-1,
    ).reshape(4, 2, rows, wide)
    other = shift(lax.dynamic_index_in_dim(total, 1 - zh, 1, False).astype(BF16), "zh", 1)

    total = lax.dynamic_index_in_dim(total, zh, 1, False) + other.astype(F32)
    total = total.astype(BF16)
    total = jnp.concatenate([total, total], axis=2)
    total = lax.dynamic_slice_in_dim(total, ((4 - zl) % 4) * depth, wide, 2)
    parts = [total[0]] + [shift(total[k], "y", -k) for k in (1, 2, 3)]
    input_grad = jnp.zeros((rows, features), BF16)
    for k in range(4):
        input_grad = lax.dynamic_update_slice(input_grad, parts[k], (0, ((y + k) % 4) * wide))

    return (input_grad, logit_grads(chances, (moving.astype(F32) + grad_w[0]) * weight_wide))


def solution(mesh):
    fine = Mesh(mesh.devices.reshape(4, 4, 4, 2, 2), ("y", "zl", "x", "zh", "c"))
    dp, tensor = ("y", "zl"), ("x", "zh", "c")
    return jax.shard_map(
        body,
        mesh=fine,
        in_specs=(
            P(dp + tensor, None),
            P(dp + tensor),
            P(dp, tensor),
            P(dp, tensor),
            P(None, dp, tensor),
            P(None, dp, tensor),
        ),
        out_specs=(P(dp + tensor, None), P(None, dp, tensor)),
        check_vma=False,
    )
```
